256 devices in a mesh: seq: 64 (over y, z, core), mp: 4 (over x).
Axes of the slice: x: 4, y: 4, z: 8, core: 2. Of those that a mesh axis runs over, the one named last changes fastest.
Arguments:
- queries: bfloat16 [512, 64, 4096], P('seq', None, 'mp'), may hold values from -5 to 5
- out_grad: bfloat16 [512, 64, 4096], P('seq', None, 'mp'), may hold values from -6 to 6
- row_keys: bfloat16 [512, 128, 4096], P('seq', None, 'mp'), may hold values from -5 to 5
- row_values: bfloat16 [512, 128, 4096], P('seq', None, 'mp'), may hold values from -6 to 6
- neighbours: int32 [512, 2], P(('seq', 'mp')), may hold values from 0 to 511, as said below
Outputs:
- query_grad: bfloat16 [512, 64, 4096], P('seq', None, 'mp')
- key_grad: bfloat16 [512, 128, 4096], P('seq', None, 'mp')
- value_grad: bfloat16 [512, 128, 4096], P('seq', None, 'mp')
The draws below stay inside these ranges and needn't reach their ends.
Inputs may be any that keep to these rules, and one draw needn't show every extreme that they name: Row r lies with seq index r // 8. The 2 neighbours of a span are different rows. The spans of one seq index retrieve at most 1 row lying with any one seq index, and some seq indices are retrieved from that often by every seq index.
All inputs are finite; a program needn't handle non-finite values.
Results may differ from the reference program's by a relative error of at most 0.008.
Values may be sent and summed in bfloat16 or wider, within the bound.
A program may use at most 320 MiB of HBM per device.

```python
import jax
import jax.numpy as jnp
from jax import lax

HEADS = 32
HEAD = 128
SPAN = 64
NLEN = 128
NBR = 2
CH_DEV = 8
ROWS_DEV = 8
OWNERS = 64
SLOT = 1
HOT = 4
SPANS = 512
ROWS = 512
WIDTH = 4096


def draw_queries(key, part):
    own_key = jax.random.fold_in(key, 11)
    return jax.random.truncated_normal(own_key, -5.0, 5.0, (SPANS, SPAN, HEADS * HEAD), jnp.float32).astype(jnp.bfloat16)


def draw_row_keys(key, part):
    own_key = jax.random.fold_in(key, 23)
    return jax.random.truncated_normal(own_key, -5.0, 5.0, (ROWS, NLEN, HEADS * HEAD), jnp.float32).astype(jnp.bfloat16)


def draw_neighbours(key, part):
    item_count = NBR * CH_DEV
    candidate_rows = OWNERS * SLOT
    own_key = jax.random.fold_in(key, 37)
    first_key, second_key, third_key, fourth_key = jax.random.split(own_key, 4)
    hot_order = jax.random.permutation(first_key, OWNERS)
    owner_rank = jnp.argsort(hot_order)
    popular_flag = owner_rank < HOT
    owning_holder = jnp.arange(candidate_rows) // SLOT
    baseline_level = jax.random.randint(second_key, (OWNERS, candidate_rows), 0, 2 ** 20)
    extra_reward = jnp.where(popular_flag[owning_holder], 2 ** 21, 0)
    ranking_score = (baseline_level + extra_reward[None, :]) * candidate_rows + jnp.arange(candidate_rows)[None, :]
    _, picked = lax.top_k(ranking_score, item_count)
    orders = jax.vmap(lambda sub_key: jax.random.permutation(sub_key, item_count))(jax.random.split(third_key, OWNERS))
    picked = jnp.take_along_axis(picked, orders, axis=1)
    owner_dev = picked // SLOT
    copy_index = picked % SLOT
    offsets = jax.random.randint(fourth_key, (OWNERS, OWNERS), 0, ROWS_DEV)
    local_row = (jnp.take_along_axis(offsets, owner_dev, axis=1) + copy_index) % ROWS_DEV
    chosen = owner_dev * ROWS_DEV + local_row
    return chosen.reshape(SPANS, NBR).astype(jnp.int32)


def levels(key, shape, pieces, smallest, top_value):
    level, own = 1.0, jax.random.fold_in(key, 6)
    for dim, parts in pieces:
        steps = jnp.exp(jax.random.uniform(jax.random.fold_in(own, dim), (parts,), jnp.float32, smallest / len(pieces), top_value / len(pieces)))
        level = level * jnp.repeat(steps, shape[dim] // parts).reshape([-1 if axis == dim else 1 for axis in range(len(shape))])
    return level


def gaussian(rng, dims, deviation, limit, cuts=(), held_as=jnp.bfloat16):
    factor_of = levels(rng, dims, cuts, -0.22, 0.18) if cuts else 1.0
    values = jax.random.normal(rng, dims, jnp.float32) * deviation * factor_of
    return jnp.minimum(jnp.maximum(values, -limit), limit).astype(held_as)


def setup_inputs(seed: int = 0) -> dict:
    keys = jax.random.split(jax.random.key(seed), 6)
    return {
        "queries": draw_queries(jax.random.fold_in(keys[5], 71), 0),
        "out_grad": gaussian(keys[1], (SPANS, SPAN, WIDTH), 1.0, 6.0, ((0, 64), (2, 4))),
        "row_keys": draw_row_keys(jax.random.fold_in(keys[5], 71), 0),
        "row_values": gaussian(keys[3], (ROWS, NLEN, WIDTH), 1.0, 6.0, ((0, 64), (2, 4))),
        "neighbours": draw_neighbours(jax.random.fold_in(keys[5], 71), 0),
    }


def span_terms(query_rows, gradient_rows, key_rows, value_rows):
    score_scale = HEAD ** -0.5
    query_f = query_rows.astype(jnp.float32).reshape(SPAN, HEADS, HEAD)
    grad_f = gradient_rows.astype(jnp.float32).reshape(SPAN, HEADS, HEAD)
    key_f = key_rows.astype(jnp.float32).reshape(NBR * NLEN, HEADS, HEAD)
    value_f = value_rows.astype(jnp.float32).reshape(NBR * NLEN, HEADS, HEAD)
    scores = jnp.einsum("ihd,jhd->hij", query_f, key_f) * score_scale
    highest = jnp.max(scores, axis=2, keepdims=True)
    log_total = highest + jnp.log(jnp.sum(jnp.exp(scores - highest), axis=2, keepdims=True))
    softmax_p = jnp.exp(scores - log_total)
    grad_p = jnp.einsum("ihd,jhd->hij", grad_f, value_f)
    row_delta = jnp.sum(softmax_p * grad_p, axis=2, keepdims=True)
    grad_low = (softmax_p * (grad_p - row_delta) * score_scale).astype(jnp.bfloat16)
    grad_s = lax.optimization_barrier(grad_low).astype(jnp.float32)
    probs_low = lax.optimization_barrier(softmax_p.astype(jnp.bfloat16)).astype(jnp.float32)
    value_part = jnp.einsum("hij,ihd->jhd", probs_low, grad_f).reshape(NBR, NLEN, HEADS * HEAD)
    key_part = jnp.einsum("hij,ihd->jhd", grad_s, query_f).reshape(NBR, NLEN, HEADS * HEAD)
    split_s = grad_s.reshape(HEADS, SPAN, NBR, NLEN)
    query_parts = jnp.einsum("hinj,njhd->nihd", split_s, key_f.reshape(NBR, NLEN, HEADS, HEAD))
    query_parts = lax.optimization_barrier(query_parts.astype(jnp.bfloat16)).astype(jnp.float32)
    query_part = jnp.sum(query_parts, axis=0).astype(jnp.bfloat16).reshape(SPAN, HEADS * HEAD)
    return query_part, key_part, value_part


def reference(queries, out_grad, row_keys, row_values, neighbours):
    def step(carry, inputs):
        key_acc, value_acc = carry
        query_rows, gradient_rows, picked = inputs
        picked = picked.astype(jnp.int32)
        key_rows = row_keys[picked].reshape(NBR * NLEN, HEADS * HEAD)
        value_rows = row_values[picked].reshape(NBR * NLEN, HEADS * HEAD)
        query_part, key_part, value_part = span_terms(query_rows, gradient_rows, key_rows, value_rows)
        key_acc = key_acc.at[picked].add(key_part)
        value_acc = value_acc.at[picked].add(value_part)
        return (key_acc, value_acc), query_part

    start = (jnp.zeros((ROWS, NLEN, HEADS * HEAD), jnp.float32), jnp.zeros((ROWS, NLEN, HEADS * HEAD), jnp.float32))
    (key_acc, value_acc), query_grad = lax.scan(step, start, (queries, out_grad, neighbours))
    return query_grad, key_acc.astype(jnp.bfloat16), value_acc.astype(jnp.bfloat16)
```

```python
import functools

import jax
import jax.numpy as jnp
from jax import lax
from jax.experimental import pallas as pl
from jax.experimental.pallas import tpu as pltpu
from jax.sharding import PartitionSpec as P

HEAD = 128
SPAN = 64
NLEN = 128
NBR = 2
NY, NZ, NC = 4, 8, 2
CH, ROWS = 8, 8
WIDE = 1024
HALF = WIDE // NC
PAIR = 2 * HEAD
PAIRS = HALF // PAIR
SOURCES = NZ * NC
SPANS_HERE = SOURCES * CH
ROWS_HERE = NY * NC * ROWS
SCALE = HEAD ** (-0.5)
LOWEST = -1e30
MESH = pl.DeviceIdType.MESH
ANY = pl.BlockSpec(memory_space=pl.ANY)
f32, bf16 = jnp.float32, jnp.bfloat16


def place():
    me = lax.axis_index("seq")
    core = lax.rem(me, NC)
    z = lax.rem(me // NC, NZ)
    y = me // (NC * NZ)
    return y, z, core


def index_of(y, z, core):
    return (lax.rem(y + NY, NY) * NZ + lax.rem(z + NZ, NZ)) * NC + core


def greet(peers):
    barrier = pltpu.get_barrier_semaphore()
    for peer in peers:
        pl.semaphore_signal(barrier, inc=1, device_id={"seq": peer}, device_id_type=MESH)
    pl.semaphore_wait(barrier, len(peers))


def remote(src, dst, send_sem, recv_sem, peer):
    return pltpu.make_async_remote_copy(
        src_ref=src, dst_ref=dst, send_sem=send_sem, recv_sem=recv_sem,
        device_id={"seq": peer}, device_id_type=MESH)


def gather_kernel(q, g, k, v, qa, ga, ka, va, loc, sib_s, sib_r, zs, zr, ys, yr):
    y, z, core = place()
    sib = index_of(y, z, 1 - core)
    z_peer = (index_of(y, z + 1, core), index_of(y, z - 1, core))
    y_peer = (index_of(y + 1, z, core), index_of(y - 1, z, core))
    greet((sib,) + z_peer + y_peer)
    own = pl.ds(pl.multiple_of(core * HALF, HALF), HALF)
    other = pl.ds(pl.multiple_of((1 - core) * HALF, HALF), HALF)
    sources = (q, g, k, v)
    gathered = (qa, ga, ka, va)
    at = (z, z, y, y)

    def z_copy(d, sub, t):
        part = core if sub == 0 else 1 - core
        block = lax.rem(z - t + NZ, NZ) if d == 0 else lax.rem(z + t, NZ)
        dst = gathered[d].at[block, part]
        src = sources[d].at[:, :, own] if (t == 0 and sub == 0) else dst
        return remote(src, dst, zs.at[d, sub, t], zr.at[d, sub, t], z_peer[d])

    def y_copy(d, sub, t):
        part = core if sub == 0 else 1 - core
        block = lax.rem(y - t + NY, NY) if d == 0 else lax.rem(y + t, NY)
        dst = gathered[2 + d].at[block, part]
        src = sources[2 + d].at[:, :, own] if (t == 0 and sub == 0) else dst
        return remote(src, dst, ys.at[d, sub, t], yr.at[d, sub, t], y_peer[d])

    sibling = [
        remote(sources[a].at[:, :, other], gathered[a].at[at[a], core], sib_s.at[a], sib_r.at[a], sib)
        for a in range(4)
    ]
    local = [
        pltpu.make_async_copy(sources[a].at[:, :, own], gathered[a].at[at[a], core], loc.at[a])
        for a in range(4)
    ]
    for d in range(2):
        z_copy(d, 0, 0).start()
    for d in range(2):
        y_copy(d, 0, 0).start()
    for copy in sibling:
        copy.start()
    for copy in local:
        copy.start()
    for d in range(2):
        sibling[d].wait_recv()
        z_copy(d, 1, 0).start()
    for d in range(2):
        sibling[2 + d].wait_recv()
        y_copy(d, 1, 0).start()

    def z_step(t):
        for sub in range(2):
            for d in range(2):
                z_copy(d, sub, t - 1).wait_recv()
                if t < NZ - 1:
                    z_copy(d, sub, t).start()

    def y_step(t):
        for sub in range(2):
            for d in range(2):
                y_copy(d, sub, t - 1).wait_recv()
                if t < NY - 1:
                    y_copy(d, sub, t).start()

    z_step(1)
    z_step(2)
    y_step(1)
    z_step(3)
    z_step(4)
    y_step(2)
    z_step(5)
    z_step(6)
    y_step(3)
    z_step(7)
    for copy in local:
        copy.wait()
    for copy in sibling:
        copy.wait_send()
    for d in range(2):
        for sub in range(2):
            for t in range(NZ - 1):
                z_copy(d, sub, t).wait_send()
            for t in range(NY - 1):
                y_copy(d, sub, t).wait_send()


def gather(q, g, k, v):
    return pl.pallas_call(
        gather_kernel,
        out_shape=(
            jax.ShapeDtypeStruct((NZ, NC, CH, SPAN, HALF), bf16),
            jax.ShapeDtypeStruct((NZ, NC, CH, SPAN, HALF), bf16),
            jax.ShapeDtypeStruct((NY, NC, ROWS, NLEN, HALF), bf16),
            jax.ShapeDtypeStruct((NY, NC, ROWS, NLEN, HALF), bf16),
        ),
        in_specs=[ANY] * 4,
        out_specs=(ANY,) * 4,
        scratch_shapes=[
            pltpu.SemaphoreType.DMA((4,)),
            pltpu.SemaphoreType.DMA((4,)),
            pltpu.SemaphoreType.DMA((4,)),
            pltpu.SemaphoreType.DMA((2, 2, NZ - 1)),
            pltpu.SemaphoreType.DMA((2, 2, NZ - 1)),
            pltpu.SemaphoreType.DMA((2, 2, NY - 1)),
            pltpu.SemaphoreType.DMA((2, 2, NY - 1)),
        ],
        compiler_params=pltpu.CompilerParams(collective_id=0, has_side_effects=True),
        name="gather_blocks",
    )(q, g, k, v)


def diagonal(ref, span, pair):
    both = ref[span, :, pl.ds(pair * PAIR, PAIR)]
    blank = jnp.zeros((SPAN, HEAD), both.dtype)
    return jnp.concatenate([
        jnp.concatenate([both[:, :HEAD], blank], axis=1),
        jnp.concatenate([blank, both[:, HEAD:]], axis=1),
    ], axis=0)


def dot(a, b, dims):
    return lax.dot_general(a, b, (dims, ((), ())), preferred_element_type=f32)


NT = ((1,), (1,))
NN = ((1,), (0,))
TN = ((0,), (0,))


def stats_kernel(near, q, g, k, v, stat, count, members):
    row = pl.program_id(0)

    @pl.when(row == 0)
    def _():
        _, z, _ = place()
        for n in range(ROWS_HERE):
            count[n] = 0

        def sort_in(item, carry):
            r = near[item]

            @pl.when(lax.rem(r // (ROWS * NC), NZ) == z)
            def _():
                slot = (r // (ROWS * NC * NZ)) * (NC * ROWS) + lax.rem(r, NC * ROWS)
                filled = count[slot]
                members[slot * SOURCES + filled] = item // NBR
                count[slot] = filled + 1

            return carry

        lax.fori_loop(0, SPANS_HERE * NBR, sort_in, 0)
        stat[:, 0] = jnp.full(stat.shape[:1] + stat.shape[2:], LOWEST, f32)
        stat[:, 1] = jnp.zeros(stat.shape[:1] + stat.shape[2:], f32)

    def item(i, carry):
        span = members[row * SOURCES + i]
        source = span // (NC * CH)
        local = lax.rem(span, NC * CH)
        tops, crosses = [], []
        for pair in range(PAIRS):
            columns = pl.ds(pair * PAIR, PAIR)
            scores = dot(k[0, :, columns], diagonal(q, span, pair), NT) * SCALE
            grad_p = dot(v[0, :, columns], diagonal(g, span, pair), NT)
            highest = jnp.max(scores, axis=0, keepdims=True)
            expons = jnp.exp(scores - highest)
            total = jnp.sum(expons, axis=0, keepdims=True)
            cross = jnp.sum(expons * grad_p, axis=0, keepdims=True)
            tops.append(highest + jnp.log(total))
            crosses.append(cross / total)
        top = jnp.concatenate(tops, axis=0)
        cross = jnp.concatenate(crosses, axis=0)
        old_top = stat[source, 0, local]
        old_cross = stat[source, 1, local]
        peak = jnp.maximum(top, old_top)
        new_w, old_w = jnp.exp(top - peak), jnp.exp(old_top - peak)
        both = new_w + old_w
        stat[source, 0, local] = peak + jnp.log(both)
        stat[source, 1, local] = (new_w * cross + old_w * old_cross) / both
        return carry

    lax.fori_loop(0, count[row], item, 0)


def whole(shape, **more):
    return pl.BlockSpec(shape, lambda *_: (0,) * len(shape), **more)


SMEM = pl.BlockSpec(memory_space=pltpu.SMEM)
ROW_BLOCK = pl.BlockSpec((1, NLEN, HALF), lambda r, *_: (r, 0, 0))
SPAN_BLOCK = whole((SPANS_HERE, SPAN, HALF), pipeline_mode=pl.Buffered(1))
STAT_SHAPE = (NZ, 2, NC * CH, PAIRS, HEAD)


def stats(near, qa, ga, ka, va):
    return pl.pallas_call(
        stats_kernel,
        grid=(ROWS_HERE,),
        out_shape=(
            jax.ShapeDtypeStruct(STAT_SHAPE, f32),
            jax.ShapeDtypeStruct((ROWS_HERE,), jnp.int32),
            jax.ShapeDtypeStruct((ROWS_HERE * SOURCES,), jnp.int32),
        ),
        in_specs=[SMEM, SPAN_BLOCK, SPAN_BLOCK, ROW_BLOCK, ROW_BLOCK],
        out_specs=(whole(STAT_SHAPE), SMEM, SMEM),
        compiler_params=pltpu.CompilerParams(vmem_limit_bytes=48 * 2**20),
        name="part_stats",
    )(near, qa, ga, ka, va)


def combine_kernel(part, full, came, send, recv, send_b, recv_b):
    y, z, core = place()
    peers = [index_of(y, z + s, core) for s in range(1, NZ)]
    greet(peers)
    out = [
        remote(part.at[lax.rem(z + s, NZ)], came.at[z], send.at[s - 1], recv.at[s - 1], peers[s - 1])
        for s in range(1, NZ)
    ]
    for copy in out:
        copy.start()
    came[z] = part[z]
    for copy in out:
        copy.wait_recv()
    tops, crosses = came[:, 0], came[:, 1]
    peak = jnp.max(tops, axis=0)
    weight = jnp.exp(tops - peak[None])
    total = jnp.sum(weight, axis=0)
    full[z, 0] = peak + jnp.log(total)
    full[z, 1] = jnp.sum(weight * crosses, axis=0) / total
    back = [
        remote(full.at[z], full.at[z], send_b.at[s - 1], recv_b.at[s - 1], peers[s - 1])
        for s in range(1, NZ)
    ]
    for copy in back:
        copy.start()
    for copy in back:
        copy.wait_recv()
    for copy in out + back:
        copy.wait_send()


def combine(part):
    vmem = pl.BlockSpec(memory_space=pltpu.VMEM)
    return pl.pallas_call(
        combine_kernel,
        out_shape=jax.ShapeDtypeStruct(STAT_SHAPE, f32),
        in_specs=[vmem],
        out_specs=vmem,
        scratch_shapes=[pltpu.VMEM(STAT_SHAPE, f32)] + [pltpu.SemaphoreType.DMA((NZ - 1,))] * 4,
        compiler_params=pltpu.CompilerParams(collective_id=1, has_side_effects=True),
        name="combine_stats",
    )(part)


def grads_kernel(count, members, q, g, k, v, stat, dq, dk, dv, dk_acc, dv_acc):
    row = pl.program_id(0)

    @pl.when(row == 0)
    def _():
        def clear(n, carry):
            dq[n] = jnp.zeros((SPAN, HALF), bf16)
            return carry

        lax.fori_loop(0, SPANS_HERE, clear, 0)

    dk_acc[...] = jnp.zeros_like(dk_acc)
    dv_acc[...] = jnp.zeros_like(dv_acc)

    def item(i, carry):
        span = members[row * SOURCES + i]
        source = span // (NC * CH)
        local = lax.rem(span, NC * CH)
        log_total = stat[source, 0, local]
        delta = stat[source, 1, local]
        for pair in range(PAIRS):
            columns = pl.ds(pair * PAIR, PAIR)
            keys, values = k[0, :, columns], v[0, :, columns]
            queries, grads = diagonal(q, span, pair), diagonal(g, span, pair)
            scores = dot(keys, queries, NT) * SCALE
            probs = jnp.exp(scores - log_total[pair:pair + 1])
            grad_p = dot(values, grads, NT)
            grad_s = (probs * (grad_p - delta[pair:pair + 1]) * SCALE).astype(bf16)
            dv_acc[:, columns] += dot(probs.astype(bf16), grads, NN)
            dk_acc[:, columns] += dot(grad_s, queries, NN)
            part = dot(grad_s, keys, TN)
            part = jnp.concatenate([part[:SPAN, :HEAD], part[SPAN:, HEAD:]], axis=1)
            part = part.astype(bf16).astype(f32)
            dq[span, :, columns] = (dq[span, :, columns].astype(f32) + part).astype(bf16)
        return carry

    lax.fori_loop(0, count[row], item, 0)
    dk[0] = dk_acc[...].astype(bf16)
    dv[0] = dv_acc[...].astype(bf16)


def grads(count, members, qa, ga, ka, va, stat):
    return pl.pallas_call(
        grads_kernel,
        grid=(ROWS_HERE,),
        out_shape=(
            jax.ShapeDtypeStruct((SPANS_HERE, SPAN, HALF), bf16),
            jax.ShapeDtypeStruct((ROWS_HERE, NLEN, HALF), bf16),
            jax.ShapeDtypeStruct((ROWS_HERE, NLEN, HALF), bf16),
        ),
        in_specs=[SMEM, SMEM, SPAN_BLOCK, SPAN_BLOCK, ROW_BLOCK, ROW_BLOCK, whole(STAT_SHAPE)],
        out_specs=(whole((SPANS_HERE, SPAN, HALF)), ROW_BLOCK, ROW_BLOCK),
        scratch_shapes=[pltpu.VMEM((NLEN, HALF), f32)] * 2,
        compiler_params=pltpu.CompilerParams(vmem_limit_bytes=56 * 2**20),
        name="part_grads",
    )(count, members, qa, ga, ka, va, stat)


def reduce_kernel(dqp, dkp, dvp, dq, dk, dv, z_in, z_own, y_in, y_own,
                  zl, yl, zs, zr, ys, yr, out_s, out_r, out_l):
    y, z, core = place()
    sib = index_of(y, z, 1 - core)
    z_peer = (index_of(y, z + 1, core), index_of(y, z - 1, core))
    y_peer = (index_of(y + 1, z, core), index_of(y - 1, z, core))
    greet((sib,) + z_peer + y_peer)
    own = pl.ds(pl.multiple_of(core * HALF, HALF), HALF)
    y_src = (dkp, dvp)
    side = (1 - core, core)

    def z_block(d, t):
        return lax.rem(z - 1 - t + 2 * NZ, NZ) if d == 0 else lax.rem(z + 1 + t, NZ)

    def y_block(d, t):
        return lax.rem(y - 1 - t + 2 * NY, NY) if d == 0 else lax.rem(y + 1 + t, NY)

    def z_copy(d, t):
        src = dqp.at[z_block(d, 0), side[d]] if t == 0 else z_in.at[d, t - 1]
        return remote(src, z_in.at[d, t], zs.at[d, t], zr.at[d, t], z_peer[d])

    def y_copy(d, sub, t):
        src = y_src[d].at[y_block(d, 0), side[sub]] if t == 0 else y_in.at[d, sub, t - 1]
        return remote(src, y_in.at[d, sub, t], ys.at[d, sub, t], yr.at[d, sub, t], y_peer[d])

    def z_load(d, t):
        return pltpu.make_async_copy(dqp.at[z_block(d, t + 1), side[d]], z_own.at[d, t], zl.at[d, t])

    def y_load(d, sub, t):
        return pltpu.make_async_copy(
            y_src[d].at[y_block(d, t + 1), side[sub]], y_own.at[d, sub, t], yl.at[d, sub, t])

    for d in range(2):
        y_copy(d, 0, 0).start()
    for d in range(2):
        z_copy(d, 0).start()
    for d in range(2):
        y_copy(d, 1, 0).start()
    for t in range(NY - 1):
        for sub in range(2):
            for d in range(2):
                y_load(d, sub, t).start()
    for t in range(NZ - 1):
        for d in range(2):
            z_load(d, t).start()

    def add(total, more, count):
        def one(n, carry):
            total[n] = (total[n].astype(f32) + more[n].astype(f32)).astype(bf16)
            return carry

        lax.fori_loop(0, count, one, 0)

    def finish(which, out, src):
        there = remote(src[0], out.at[:, :, own], out_s.at[which], out_r.at[which], sib)
        here = pltpu.make_async_copy(src[1], out.at[:, :, own], out_l.at[which])
        return there, here

    ends = (
        finish(0, dk, (y_in.at[0, 0, NY - 2], y_in.at[0, 1, NY - 2])),
        finish(1, dv, (y_in.at[1, 0, NY - 2], y_in.at[1, 1, NY - 2])),
        finish(2, dq, (z_in.at[0, NZ - 2], z_in.at[1, NZ - 2])),
    )

    def z_step(t):
        for d in range(2):
            z_copy(d, t).wait_recv()
            z_load(d, t).wait()
            add(z_in.at[d, t], z_own.at[d, t], CH)
            if t < NZ - 2:
                z_copy(d, t + 1).start()
            else:
                ends[2][d].start()

    def y_step(t, sub):
        for d in range(2):
            y_copy(d, sub, t).wait_recv()
            y_load(d, sub, t).wait()
            add(y_in.at[d, sub, t], y_own.at[d, sub, t], ROWS)
            if t < NY - 2:
                y_copy(d, sub, t + 1).start()
            else:
                ends[d][sub].start()

    z_step(0)
    y_step(0, 0)
    z_step(1)
    y_step(0, 1)
    z_step(2)
    y_step(1, 0)
    z_step(3)
    z_step(4)
    y_step(1, 1)
    z_step(5)
    y_step(2, 0)
    z_step(6)
    y_step(2, 1)
    for there, here in ends:
        there.wait()
        here.wait()
    for d in range(2):
        for t in range(NZ - 1):
            z_copy(d, t).wait_send()
        for sub in range(2):
            for t in range(NY - 1):
                y_copy(d, sub, t).wait_send()


def reduce(dqp, dkp, dvp):
    sem = pltpu.SemaphoreType.DMA
    return pl.pallas_call(
        reduce_kernel,
        out_shape=(
            jax.ShapeDtypeStruct((CH, SPAN, WIDE), bf16),
            jax.ShapeDtypeStruct((ROWS, NLEN, WIDE), bf16),
            jax.ShapeDtypeStruct((ROWS, NLEN, WIDE), bf16),
        ),
        in_specs=[ANY] * 3,
        out_specs=(ANY,) * 3,
        scratch_shapes=[
            pltpu.VMEM((2, NZ - 1, CH, SPAN, HALF), bf16),
            pltpu.VMEM((2, NZ - 1, CH, SPAN, HALF), bf16),
            pltpu.VMEM((2, 2, NY - 1, ROWS, NLEN, HALF), bf16),
            pltpu.VMEM((2, 2, NY - 1, ROWS, NLEN, HALF), bf16),
            sem((2, NZ - 1)),
            sem((2, 2, NY - 1)),
            sem((2, NZ - 1)),
            sem((2, NZ - 1)),
            sem((2, 2, NY - 1)),
            sem((2, 2, NY - 1)),
            sem((3,)),
            sem((3,)),
            sem((3,)),
        ],
        compiler_params=pltpu.CompilerParams(
            collective_id=2, has_side_effects=True, vmem_limit_bytes=56 * 2**20),
        name="reduce_blocks",
    )(dqp, dkp, dvp)


def per_device(queries, out_grad, row_keys, row_values, neighbours):
    y, _, _ = place()
    lists = lax.all_gather(neighbours, ("seq", "mp"), axis=0, tiled=True)
    near = lax.dynamic_slice_in_dim(lists, y * SPANS_HERE, SPANS_HERE, 0).reshape(-1)
    qa, ga, ka, va = gather(queries, out_grad, row_keys, row_values)
    qa = qa.reshape(SPANS_HERE, SPAN, HALF)
    ga = ga.reshape(SPANS_HERE, SPAN, HALF)
    ka = ka.reshape(ROWS_HERE, NLEN, HALF)
    va = va.reshape(ROWS_HERE, NLEN, HALF)
    part, count, members = stats(near, qa, ga, ka, va)
    full = combine(part)
    dqp, dkp, dvp = grads(count, members, qa, ga, ka, va, full)
    return reduce(
        dqp.reshape(NZ, NC, CH, SPAN, HALF),
        dkp.reshape(NY, NC, ROWS, NLEN, HALF),
        dvp.reshape(NY, NC, ROWS, NLEN, HALF),
    )


def solution(mesh):
    in_specs = (
        P("seq", None, "mp"),
        P("seq", None, "mp"),
        P("seq", None, "mp"),
        P("seq", None, "mp"),
        P(("seq", "mp"), None),
    )
    out_specs = (P("seq", None, "mp"), P("seq", None, "mp"), P("seq", None, "mp"))
    return jax.shard_map(
        per_device, mesh=mesh, in_specs=in_specs, out_specs=out_specs, check_vma=False
    )
```

```python
import functools

import jax
import jax.numpy as jnp
from jax import lax
from jax.experimental import pallas as pl
from jax.experimental.pallas import tpu as pltpu
from jax.sharding import PartitionSpec as P

HEAD = 128
SPAN = 64
NLEN = 128
NBR = 2
NX, NY, NZ, NC = 4, 4, 8, 2
CH, ROWS = 8, 8
WIDE = 1024
HALF = WIDE // NC
PAIR = 2 * HEAD
PAIRS = HALF // PAIR
SOURCES = NZ * NC
SPANS_HERE = SOURCES * CH
OWNERS_HERE = NY * NC
ROWS_HERE = OWNERS_HERE * ROWS
SCALE = HEAD ** (-0.5)
LOWEST = -1e30
MESH = pl.DeviceIdType.MESH
ANY = pl.BlockSpec(memory_space=pl.ANY)
f32, bf16 = jnp.float32, jnp.bfloat16


def place():
    me = lax.axis_index("seq")
    core = lax.rem(me, NC)
    z = lax.rem(me // NC, NZ)
    y = me // (NC * NZ)
    return y, z, core


def index_of(y, z, core):
    return (lax.rem(y + NY, NY) * NZ + lax.rem(z + NZ, NZ)) * NC + core


def greet(peers):
    barrier = pltpu.get_barrier_semaphore()
    for peer in peers:
        pl.semaphore_signal(barrier, inc=1, device_id={"seq": peer}, device_id_type=MESH)
    pl.semaphore_wait(barrier, len(peers))


def remote(src, dst, send_sem, recv_sem, peer):
    return pltpu.make_async_remote_copy(
        src_ref=src, dst_ref=dst, send_sem=send_sem, recv_sem=recv_sem,
        device_id={"seq": peer}, device_id_type=MESH)


def gather_kernel(q, g, k, v, lists, qa, ga, ka, va, near, loc, sib_s, sib_r, zs, zr, ys, yr,
                  near_s, near_r):
    y, z, core = place()
    mp = lax.axis_index("mp")
    sib = index_of(y, z, 1 - core)
    z_peer = (index_of(y, z + 1, core), index_of(y, z - 1, core))
    y_peer = (index_of(y + 1, z, core), index_of(y - 1, z, core))
    line = [index_of(y, z + s, core) for s in range(1, NZ)]
    line += [index_of(y, z + s, 1 - core) for s in range(NZ)]
    barrier = pltpu.get_barrier_semaphore()
    for s in range(1, NX):
        pl.semaphore_signal(
            barrier, inc=1, device_id={"mp": lax.rem(mp + s, NX)}, device_id_type=MESH)
    for peer in line + list(y_peer):
        pl.semaphore_signal(barrier, inc=1, device_id={"seq": peer}, device_id_type=MESH)
    pl.semaphore_wait(barrier, NX - 1 + len(line) + len(y_peer))
    mine = z * NC + core
    near_x = [
        pltpu.make_async_remote_copy(
            src_ref=lists, dst_ref=near.at[mine, mp], send_sem=near_s.at[s - 1],
            recv_sem=near_r.at[s - 1], device_id={"mp": lax.rem(mp + s, NX)}, device_id_type=MESH)
        for s in range(1, NX)
    ]
    near_line = [
        remote(near.at[mine], near.at[mine], near_s.at[NX - 1 + n], near_r.at[NX - 1 + n], peer)
        for n, peer in enumerate(line)
    ]
    own = pl.ds(pl.multiple_of(core * HALF, HALF), HALF)
    other = pl.ds(pl.multiple_of((1 - core) * HALF, HALF), HALF)
    sources = (q, g, k, v)
    gathered = (qa, ga, ka, va)
    at = (z, z, y, y)

    def z_copy(d, sub, t):
        part = core if sub == 0 else 1 - core
        block = lax.rem(z - t + NZ, NZ) if d == 0 else lax.rem(z + t, NZ)
        dst = gathered[d].at[block, part]
        src = sources[d].at[:, :, own] if (t == 0 and sub == 0) else dst
        return remote(src, dst, zs.at[d, sub, t], zr.at[d, sub, t], z_peer[d])

    def y_copy(d, sub, t):
        part = core if sub == 0 else 1 - core
        block = lax.rem(y - t + NY, NY) if d == 0 else lax.rem(y + t, NY)
        dst = gathered[2 + d].at[block, part]
        src = sources[2 + d].at[:, :, own] if (t == 0 and sub == 0) else dst
        return remote(src, dst, ys.at[d, sub, t], yr.at[d, sub, t], y_peer[d])

    sibling = [
        remote(sources[a].at[:, :, other], gathered[a].at[at[a], core], sib_s.at[a], sib_r.at[a], sib)
        for a in range(4)
    ]
    local = [
        pltpu.make_async_copy(sources[a].at[:, :, own], gathered[a].at[at[a], core], loc.at[a])
        for a in range(4)
    ]
    for d in range(2):
        z_copy(d, 0, 0).start()
    for d in range(2):
        y_copy(d, 0, 0).start()
    for copy in sibling:
        copy.start()
    for copy in near_x:
        copy.start()
    for copy in local:
        copy.start()
    near[mine, mp] = lists[...]
    for d in range(2):
        sibling[d].wait_recv()
        z_copy(d, 1, 0).start()
    for d in range(2):
        sibling[2 + d].wait_recv()
        y_copy(d, 1, 0).start()

    for copy in near_x:
        copy.wait_recv()
    for copy in near_line:
        copy.start()

    def z_step(t):
        for sub in range(2):
            for d in range(2):
                z_copy(d, sub, t - 1).wait_recv()
                if t < NZ - 1:
                    z_copy(d, sub, t).start()

    def y_step(t):
        for sub in range(2):
            for d in range(2):
                y_copy(d, sub, t - 1).wait_recv()
                if t < NY - 1:
                    y_copy(d, sub, t).start()

    z_step(1)
    z_step(2)
    y_step(1)
    z_step(3)
    z_step(4)
    y_step(2)
    z_step(5)
    z_step(6)
    y_step(3)
    z_step(7)
    for copy in near_line:
        copy.wait_recv()
    for copy in near_x + near_line:
        copy.wait_send()
    for copy in local:
        copy.wait()
    for copy in sibling:
        copy.wait_send()
    for d in range(2):
        for sub in range(2):
            for t in range(NZ - 1):
                z_copy(d, sub, t).wait_send()
            for t in range(NY - 1):
                y_copy(d, sub, t).wait_send()


def gather(q, g, k, v, lists):
    sem = pltpu.SemaphoreType.DMA
    vmem = pl.BlockSpec(memory_space=pltpu.VMEM)
    return pl.pallas_call(
        gather_kernel,
        out_shape=(
            jax.ShapeDtypeStruct((NZ, NC, CH, SPAN, HALF), bf16),
            jax.ShapeDtypeStruct((NZ, NC, CH, SPAN, HALF), bf16),
            jax.ShapeDtypeStruct((NY, NC, ROWS, NLEN, HALF), bf16),
            jax.ShapeDtypeStruct((NY, NC, ROWS, NLEN, HALF), bf16),
            jax.ShapeDtypeStruct((SOURCES, NX, 1, 128), jnp.int32),
        ),
        in_specs=[ANY] * 4 + [vmem],
        out_specs=(ANY,) * 4 + (vmem,),
        scratch_shapes=[
            sem((4,)),
            sem((4,)),
            sem((4,)),
            sem((2, 2, NZ - 1)),
            sem((2, 2, NZ - 1)),
            sem((2, 2, NY - 1)),
            sem((2, 2, NY - 1)),
            sem((NX - 1 + SOURCES - 1,)),
            sem((NX - 1 + SOURCES - 1,)),
        ],
        compiler_params=pltpu.CompilerParams(collective_id=0, has_side_effects=True),
        name="gather_blocks",
    )(q, g, k, v, lists)


def diagonal(ref, span, pair):
    both = ref[span, :, pl.ds(pair * PAIR, PAIR)]
    blank = jnp.zeros((SPAN, HEAD), both.dtype)
    return jnp.concatenate([
        jnp.concatenate([both[:, :HEAD], blank], axis=1),
        jnp.concatenate([blank, both[:, HEAD:]], axis=1),
    ], axis=0)


def dot(a, b, dims):
    return lax.dot_general(a, b, (dims, ((), ())), preferred_element_type=f32)


NT = ((1,), (1,))
NN = ((1,), (0,))
TN = ((0,), (0,))


def stats_kernel(near, q, g, k, v, stat, count, members):
    owner = pl.program_id(0)

    @pl.when(owner == 0)
    def _():
        _, z, _ = place()
        for n in range(OWNERS_HERE):
            count[n] = 0

        def sort_in(item, carry):
            r = near[item]

            @pl.when(lax.rem(r // (ROWS * NC), NZ) == z)
            def _():
                slot = (r // (ROWS * NC * NZ)) * NC + lax.rem(r // ROWS, NC)
                filled = count[slot]
                members[slot * SOURCES + filled] = (item // NBR) * ROWS + lax.rem(r, ROWS)
                count[slot] = filled + 1

            return carry

        lax.fori_loop(0, SPANS_HERE * NBR, sort_in, 0)
        stat[:, 0] = jnp.full(stat.shape[:1] + stat.shape[2:], LOWEST, f32)
        stat[:, 1] = jnp.zeros(stat.shape[:1] + stat.shape[2:], f32)

    def item(i, carry):
        member = members[owner * SOURCES + i]
        span, row = member // ROWS, lax.rem(member, ROWS)
        source = span // (NC * CH)
        local = lax.rem(span, NC * CH)
        tops, crosses = [], []
        for pair in range(PAIRS):
            columns = pl.ds(pair * PAIR, PAIR)
            scores = dot(k[row, :, columns], diagonal(q, span, pair), NT) * SCALE
            grad_p = dot(v[row, :, columns], diagonal(g, span, pair), NT)
            highest = jnp.max(scores, axis=0, keepdims=True)
            expons = jnp.exp(scores - highest)
            total = jnp.sum(expons, axis=0, keepdims=True)
            cross = jnp.sum(expons * grad_p, axis=0, keepdims=True)
            tops.append(highest + jnp.log(total))
            crosses.append(cross / total)
        top = jnp.concatenate(tops, axis=0)
        cross = jnp.concatenate(crosses, axis=0)
        old_top = stat[source, 0, local]
        old_cross = stat[source, 1, local]
        peak = jnp.maximum(top, old_top)
        new_w, old_w = jnp.exp(top - peak), jnp.exp(old_top - peak)
        both = new_w + old_w
        stat[source, 0, local] = peak + jnp.log(both)
        stat[source, 1, local] = (new_w * cross + old_w * old_cross) / both
        return carry

    lax.fori_loop(0, count[owner], item, 0)


def whole(shape, **more):
    return pl.BlockSpec(shape, lambda *_: (0,) * len(shape), **more)


SMEM = pl.BlockSpec(memory_space=pltpu.SMEM)
ROW_BLOCK = pl.BlockSpec((ROWS, NLEN, HALF), lambda n: (n, 0, 0))
SPAN_BLOCK = whole((SPANS_HERE, SPAN, HALF), pipeline_mode=pl.Buffered(1))
STAT_SHAPE = (NZ, 2, NC * CH, PAIRS, HEAD)


def stats(near, qa, ga, ka, va):
    return pl.pallas_call(
        stats_kernel,
        grid=(OWNERS_HERE,),
        out_shape=(
            jax.ShapeDtypeStruct(STAT_SHAPE, f32),
            jax.ShapeDtypeStruct((OWNERS_HERE,), jnp.int32),
            jax.ShapeDtypeStruct((OWNERS_HERE * SOURCES,), jnp.int32),
        ),
        in_specs=[SMEM, SPAN_BLOCK, SPAN_BLOCK, ROW_BLOCK, ROW_BLOCK],
        out_specs=(whole(STAT_SHAPE), SMEM, SMEM),
        compiler_params=pltpu.CompilerParams(vmem_limit_bytes=48 * 2**20),
        name="part_stats",
    )(near, qa, ga, ka, va)


def combine_kernel(part, full, came, send, recv, send_b, recv_b):
    y, z, core = place()
    peers = [index_of(y, z + s, core) for s in range(1, NZ)]
    greet(peers)
    out = [
        remote(part.at[lax.rem(z + s, NZ)], came.at[z], send.at[s - 1], recv.at[s - 1], peers[s - 1])
        for s in range(1, NZ)
    ]
    for copy in out:
        copy.start()
    came[z] = part[z]
    for copy in out:
        copy.wait_recv()
    tops, crosses = came[:, 0], came[:, 1]
    peak = jnp.max(tops, axis=0)
    weight = jnp.exp(tops - peak[None])
    total = jnp.sum(weight, axis=0)
    full[z, 0] = peak + jnp.log(total)
    full[z, 1] = jnp.sum(weight * crosses, axis=0) / total
    back = [
        remote(full.at[z], full.at[z], send_b.at[s - 1], recv_b.at[s - 1], peers[s - 1])
        for s in range(1, NZ)
    ]
    for copy in back:
        copy.start()
    for copy in back:
        copy.wait_recv()
    for copy in out + back:
        copy.wait_send()


def combine(part):
    vmem = pl.BlockSpec(memory_space=pltpu.VMEM)
    return pl.pallas_call(
        combine_kernel,
        out_shape=jax.ShapeDtypeStruct(STAT_SHAPE, f32),
        in_specs=[vmem],
        out_specs=vmem,
        scratch_shapes=[pltpu.VMEM(STAT_SHAPE, f32)] + [pltpu.SemaphoreType.DMA((NZ - 1,))] * 4,
        compiler_params=pltpu.CompilerParams(collective_id=1, has_side_effects=True),
        name="combine_stats",
    )(part)


def grads_kernel(count, members, q, g, k, v, stat, dq, dk, dv, dk_acc, dv_acc):
    owner = pl.program_id(0)

    @pl.when(owner == 0)
    def _():
        def clear(n, carry):
            dq[n] = jnp.zeros((SPAN, HALF), bf16)
            return carry

        lax.fori_loop(0, SPANS_HERE, clear, 0)

    def fresh(n, carry):
        dk_acc[n] = jnp.zeros((NLEN, HALF), f32)
        dv_acc[n] = jnp.zeros((NLEN, HALF), f32)
        return carry

    lax.fori_loop(0, ROWS, fresh, 0)

    def item(i, carry):
        member = members[owner * SOURCES + i]
        span, row = member // ROWS, lax.rem(member, ROWS)
        source = span // (NC * CH)
        local = lax.rem(span, NC * CH)
        log_total = stat[source, 0, local]
        delta = stat[source, 1, local]
        for pair in range(PAIRS):
            columns = pl.ds(pair * PAIR, PAIR)
            keys, values = k[row, :, columns], v[row, :, columns]
            queries, grads = diagonal(q, span, pair), diagonal(g, span, pair)
            scores = dot(keys, queries, NT) * SCALE
            probs = jnp.exp(scores - log_total[pair:pair + 1])
            grad_p = dot(values, grads, NT)
            grad_s = (probs * (grad_p - delta[pair:pair + 1]) * SCALE).astype(bf16)
            dv_acc[row, :, columns] += dot(probs.astype(bf16), grads, NN)
            dk_acc[row, :, columns] += dot(grad_s, queries, NN)
            part = dot(grad_s, keys, TN)
            part = jnp.concatenate([part[:SPAN, :HEAD], part[SPAN:, HEAD:]], axis=1)
            part = part.astype(bf16).astype(f32)
            dq[span, :, columns] = (dq[span, :, columns].astype(f32) + part).astype(bf16)
        return carry

    lax.fori_loop(0, count[owner], item, 0)

    def settle(n, carry):
        dk[n] = dk_acc[n].astype(bf16)
        dv[n] = dv_acc[n].astype(bf16)
        return carry

    lax.fori_loop(0, ROWS, settle, 0)


def grads(count, members, qa, ga, ka, va, stat):
    return pl.pallas_call(
        grads_kernel,
        grid=(OWNERS_HERE,),
        out_shape=(
            jax.ShapeDtypeStruct((SPANS_HERE, SPAN, HALF), bf16),
            jax.ShapeDtypeStruct((ROWS_HERE, NLEN, HALF), bf16),
            jax.ShapeDtypeStruct((ROWS_HERE, NLEN, HALF), bf16),
        ),
        in_specs=[SMEM, SMEM, SPAN_BLOCK, SPAN_BLOCK, ROW_BLOCK, ROW_BLOCK, whole(STAT_SHAPE)],
        out_specs=(whole((SPANS_HERE, SPAN, HALF)), ROW_BLOCK, ROW_BLOCK),
        scratch_shapes=[pltpu.VMEM((ROWS, NLEN, HALF), f32)] * 2,
        compiler_params=pltpu.CompilerParams(vmem_limit_bytes=56 * 2**20),
        name="part_grads",
    )(count, members, qa, ga, ka, va, stat)


def reduce_kernel(dqp, dkp, dvp, dq, dk, dv, z_in, z_own, y_in, y_own,
                  zl, yl, zs, zr, ys, yr, out_s, out_r, out_l):
    y, z, core = place()
    sib = index_of(y, z, 1 - core)
    z_peer = (index_of(y, z + 1, core), index_of(y, z - 1, core))
    y_peer = (index_of(y + 1, z, core), index_of(y - 1, z, core))
    greet((sib,) + z_peer + y_peer)
    own = pl.ds(pl.multiple_of(core * HALF, HALF), HALF)
    y_src = (dkp, dvp)
    side = (1 - core, core)

    def z_block(d, t):
        return lax.rem(z - 1 - t + 2 * NZ, NZ) if d == 0 else lax.rem(z + 1 + t, NZ)

    def y_block(d, t):
        return lax.rem(y - 1 - t + 2 * NY, NY) if d == 0 else lax.rem(y + 1 + t, NY)

    def z_copy(d, t):
        src = dqp.at[z_block(d, 0), side[d]] if t == 0 else z_in.at[d, t - 1]
        return remote(src, z_in.at[d, t], zs.at[d, t], zr.at[d, t], z_peer[d])

    def y_copy(d, sub, t):
        src = y_src[d].at[y_block(d, 0), side[sub]] if t == 0 else y_in.at[d, sub, t - 1]
        return remote(src, y_in.at[d, sub, t], ys.at[d, sub, t], yr.at[d, sub, t], y_peer[d])

    def z_load(d, t):
        return pltpu.make_async_copy(dqp.at[z_block(d, t + 1), side[d]], z_own.at[d, t], zl.at[d, t])

    def y_load(d, sub, t):
        return pltpu.make_async_copy(
            y_src[d].at[y_block(d, t + 1), side[sub]], y_own.at[d, sub, t], yl.at[d, sub, t])

    for d in range(2):
        y_copy(d, 0, 0).start()
    for d in range(2):
        z_copy(d, 0).start()
    for d in range(2):
        y_copy(d, 1, 0).start()
    for t in range(NY - 1):
        for sub in range(2):
            for d in range(2):
                y_load(d, sub, t).start()
    for t in range(NZ - 1):
        for d in range(2):
            z_load(d, t).start()

    def add(total, more, count):
        def one(n, carry):
            total[n] = (total[n].astype(f32) + more[n].astype(f32)).astype(bf16)
            return carry

        lax.fori_loop(0, count, one, 0)

    def finish(which, out, src):
        there = remote(src[0], out.at[:, :, own], out_s.at[which], out_r.at[which], sib)
        here = pltpu.make_async_copy(src[1], out.at[:, :, own], out_l.at[which])
        return there, here

    ends = (
        finish(0, dk, (y_in.at[0, 0, NY - 2], y_in.at[0, 1, NY - 2])),
        finish(1, dv, (y_in.at[1, 0, NY - 2], y_in.at[1, 1, NY - 2])),
        finish(2, dq, (z_in.at[0, NZ - 2], z_in.at[1, NZ - 2])),
    )

    def z_step(t):
        for d in range(2):
            z_copy(d, t).wait_recv()
            z_load(d, t).wait()
            add(z_in.at[d, t], z_own.at[d, t], CH)
            if t < NZ - 2:
                z_copy(d, t + 1).start()
            else:
                ends[2][d].start()

    def y_step(t, sub):
        for d in range(2):
            y_copy(d, sub, t).wait_recv()
            y_load(d, sub, t).wait()
            add(y_in.at[d, sub, t], y_own.at[d, sub, t], ROWS)
            if t < NY - 2:
                y_copy(d, sub, t + 1).start()
            else:
                ends[d][sub].start()

    z_step(0)
    y_step(0, 0)
    z_step(1)
    y_step(0, 1)
    z_step(2)
    y_step(1, 0)
    z_step(3)
    z_step(4)
    y_step(1, 1)
    z_step(5)
    y_step(2, 0)
    z_step(6)
    y_step(2, 1)
    for there, here in ends:
        there.wait()
        here.wait()
    for d in range(2):
        for t in range(NZ - 1):
            z_copy(d, t).wait_send()
        for sub in range(2):
            for t in range(NY - 1):
                y_copy(d, sub, t).wait_send()


def reduce(dqp, dkp, dvp):
    sem = pltpu.SemaphoreType.DMA
    return pl.pallas_call(
        reduce_kernel,
        out_shape=(
            jax.ShapeDtypeStruct((CH, SPAN, WIDE), bf16),
            jax.ShapeDtypeStruct((ROWS, NLEN, WIDE), bf16),
            jax.ShapeDtypeStruct((ROWS, NLEN, WIDE), bf16),
        ),
        in_specs=[ANY] * 3,
        out_specs=(ANY,) * 3,
        scratch_shapes=[
            pltpu.VMEM((2, NZ - 1, CH, SPAN, HALF), bf16),
            pltpu.VMEM((2, NZ - 1, CH, SPAN, HALF), bf16),
            pltpu.VMEM((2, 2, NY - 1, ROWS, NLEN, HALF), bf16),
            pltpu.VMEM((2, 2, NY - 1, ROWS, NLEN, HALF), bf16),
            sem((2, NZ - 1)),
            sem((2, 2, NY - 1)),
            sem((2, NZ - 1)),
            sem((2, NZ - 1)),
            sem((2, 2, NY - 1)),
            sem((2, 2, NY - 1)),
            sem((3,)),
            sem((3,)),
            sem((3,)),
        ],
        compiler_params=pltpu.CompilerParams(
            collective_id=2, has_side_effects=True, vmem_limit_bytes=56 * 2**20),
        name="reduce_blocks",
    )(dqp, dkp, dvp)


def per_device(queries, out_grad, row_keys, row_values, neighbours):
    few = neighbours.size
    lists = jnp.pad(neighbours.reshape(1, few), ((0, 0), (0, 128 - few)))
    qa, ga, ka, va, near = gather(queries, out_grad, row_keys, row_values, lists)
    near = near[:, :, 0, :few].reshape(-1)
    qa = qa.reshape(SPANS_HERE, SPAN, HALF)
    ga = ga.reshape(SPANS_HERE, SPAN, HALF)
    ka = ka.reshape(ROWS_HERE, NLEN, HALF)
    va = va.reshape(ROWS_HERE, NLEN, HALF)
    part, count, members = stats(near, qa, ga, ka, va)
    full = combine(part)
    dqp, dkp, dvp = grads(count, members, qa, ga, ka, va, full)
    return reduce(
        dqp.reshape(NZ, NC, CH, SPAN, HALF),
        dkp.reshape(NY, NC, ROWS, NLEN, HALF),
        dvp.reshape(NY, NC, ROWS, NLEN, HALF),
    )


def solution(mesh):
    in_specs = (
        P("seq", None, "mp"),
        P("seq", None, "mp"),
        P("seq", None, "mp"),
        P("seq", None, "mp"),
        P(("seq", "mp"), None),
    )
    out_specs = (P("seq", None, "mp"), P("seq", None, "mp"), P("seq", None, "mp"))
    return jax.shard_map(
        per_device, mesh=mesh, in_specs=in_specs, out_specs=out_specs, check_vma=False
    )
```

```python
import jax
import jax.numpy as jnp
from jax import lax
from jax.experimental import pallas as pl
from jax.experimental.pallas import tpu as pltpu
from jax.sharding import PartitionSpec as P

HEAD = 128
SPAN = 64
NLEN = 128
NBR = 2
NX, NY, NZ, NC = 4, 4, 8, 2
CH, ROWS = 8, 8
WIDE = 1024
HALF = WIDE // NC
PAIR = 2 * HEAD
PAIRS = HALF // PAIR
SOURCES = NZ * NC
SPANS_HERE = SOURCES * CH
OWNERS_HERE = NY * NC
ROWS_HERE = OWNERS_HERE * ROWS
SCALE = HEAD ** (-0.5)
MESH = pl.DeviceIdType.MESH
ANY = pl.BlockSpec(memory_space=pl.ANY)
f32, bf16 = jnp.float32, jnp.bfloat16


def place():
    me = lax.axis_index("seq")
    core = lax.rem(me, NC)
    z = lax.rem(me // NC, NZ)
    y = me // (NC * NZ)
    return y, z, core


def index_of(y, z, core):
    return (lax.rem(y + NY, NY) * NZ + lax.rem(z + NZ, NZ)) * NC + core


def greet(peers):
    barrier = pltpu.get_barrier_semaphore()
    for peer in peers:
        pl.semaphore_signal(barrier, inc=1, device_id={"seq": peer}, device_id_type=MESH)
    pl.semaphore_wait(barrier, len(peers))


def remote(src, dst, send_sem, recv_sem, peer):
    return pltpu.make_async_remote_copy(
        src_ref=src, dst_ref=dst, send_sem=send_sem, recv_sem=recv_sem,
        device_id={"seq": peer}, device_id_type=MESH)


NT = ((1,), (1,))
NN = ((1,), (0,))
TN = ((0,), (0,))


def dot(a, b, dims):
    return lax.dot_general(a, b, (dims, ((), ())), preferred_element_type=f32)


def diagonal(both):
    blank = jnp.zeros((SPAN, HEAD), both.dtype)
    return jnp.concatenate([
        jnp.concatenate([both[:, :HEAD], blank], axis=1),
        jnp.concatenate([blank, both[:, HEAD:]], axis=1),
    ], axis=0)


def gather_kernel(q, g, k, v, lists, qa, ga, ka, va, table, hits, full,
                  qc, gc, kc, vc, near, near_sm, part, came,
                  own_l, sib_s, sib_r, zs, zr, ys, yr, near_s, near_r, near_l, z_load, y_load,
                  part_s, part_r, full_s, full_r):
    y, z, core = place()
    mp = lax.axis_index("mp")
    sib = index_of(y, z, 1 - core)
    z_peer = (index_of(y, z + 1, core), index_of(y, z - 1, core))
    y_peer = (index_of(y + 1, z, core), index_of(y - 1, z, core))
    line = [index_of(y, z + s, core) for s in range(1, NZ)]
    line += [index_of(y, z + s, 1 - core) for s in range(NZ)]
    barrier = pltpu.get_barrier_semaphore()
    for s in range(1, NX):
        pl.semaphore_signal(
            barrier, inc=1, device_id={"mp": lax.rem(mp + s, NX)}, device_id_type=MESH)
    for peer in line + list(y_peer):
        pl.semaphore_signal(barrier, inc=1, device_id={"seq": peer}, device_id_type=MESH)
    pl.semaphore_wait(barrier, NX - 1 + len(line) + len(y_peer))
    mine = z * NC + core
    near_x = [
        pltpu.make_async_remote_copy(
            src_ref=lists, dst_ref=near.at[mine, mp], send_sem=near_s.at[s - 1],
            recv_sem=near_r.at[s - 1], device_id={"mp": lax.rem(mp + s, NX)}, device_id_type=MESH)
        for s in range(1, NX)
    ]
    near_line = [
        remote(near.at[mine], near.at[mine], near_s.at[NX - 1 + n], near_r.at[NX - 1 + n], peer)
        for n, peer in enumerate(line)
    ]
    own = pl.ds(pl.multiple_of(core * HALF, HALF), HALF)
    other = pl.ds(pl.multiple_of((1 - core) * HALF, HALF), HALF)
    sources = (q, g, k, v)
    gathered = (qa, ga, ka, va)
    here = (qc, gc, kc, vc)
    side = (core, 1 - core)

    def z_at(d, t):
        return lax.rem(z + (2 * d - 1) * t + NZ, NZ)

    def y_at(d, t):
        return lax.rem(y + (2 * d - 1) * t + NY, NY)

    def z_copy(d, a, t):
        dst = gathered[a].at[z_at(d, t), side[d]]
        src = sources[a].at[:, :, own] if (t == 0 and d == 0) else dst
        return remote(src, dst, zs.at[d, a, t], zr.at[d, a, t], z_peer[d])

    def y_copy(d, a, t):
        dst = gathered[2 + a].at[y_at(d, t), side[d]]
        src = sources[2 + a].at[:, :, own] if (t == 0 and d == 0) else dst
        return remote(src, dst, ys.at[d, a, t], yr.at[d, a, t], y_peer[d])

    def z_in(d, a, t):
        src = sources[a].at[:, :, own] if (t == 0 and d == 0) else gathered[a].at[z_at(d, t), side[d]]
        return pltpu.make_async_copy(src, here[a].at[z_at(d, t) * NC + side[d]], z_load.at[d, a, t])

    def y_in(d, a, t):
        src = sources[2 + a].at[:, :, own] if (t == 0 and d == 0) else gathered[2 + a].at[y_at(d, t), side[d]]
        return pltpu.make_async_copy(src, here[2 + a].at[y_at(d, t) * NC + side[d]], y_load.at[d, a, t])

    at = (z, z, y, y)
    sibling = [
        remote(sources[a].at[:, :, other], gathered[a].at[at[a], core], sib_s.at[a], sib_r.at[a], sib)
        for a in range(4)
    ]
    for a in range(2):
        z_copy(0, a, 0).start()
    for copy in sibling[:2]:
        copy.start()
    for a in range(2):
        y_copy(0, a, 0).start()
    for copy in sibling[2:]:
        copy.start()
    for copy in near_x:
        copy.start()
    local = [
        pltpu.make_async_copy(sources[a].at[:, :, own], gathered[a].at[at[a], core], own_l.at[a])
        for a in range(4)
    ]
    for copy in local:
        copy.start()
    for a in range(2):
        z_in(0, a, 0).start()
        y_in(0, a, 0).start()
    near[mine, mp] = lists[...]
    for a in range(2):
        sibling[a].wait_recv()
        z_copy(1, a, 0).start()
        z_in(1, a, 0).start()
    for a in range(2):
        sibling[2 + a].wait_recv()
        y_copy(1, a, 0).start()
        y_in(1, a, 0).start()
    for copy in near_x:
        copy.wait_recv()
    for copy in near_line:
        copy.start()
    for copy in near_line:
        copy.wait_recv()
    listed = pltpu.make_async_copy(near, near_sm, near_l)
    listed.start()
    listed.wait()

    def look_up(slot, carry):
        source, owner = slot // OWNERS_HERE, lax.rem(slot, OWNERS_HERE)
        wanted = ((owner // NC) * NZ + z) * NC + lax.rem(owner, NC)
        found = jnp.int32(0)
        hit = jnp.int32(0)
        for item in range(CH * NBR):
            r = near_sm[source, item // (CH * NBR // NX), 0, item % (CH * NBR // NX)]
            same = (r // ROWS == wanted).astype(jnp.int32)
            found = found + same * (item // NBR * ROWS + lax.rem(r, ROWS) - found)
            hit = hit + same
        table[slot] = found
        hits[slot] = hit
        return carry

    lax.fori_loop(0, SOURCES * OWNERS_HERE, look_up, 0)

    def part_stats(first_source, last_source, first_owner, last_owner):
        owners = last_owner - first_owner

        def one(n, carry):
            a = first_source + n // owners
            b = first_owner + lax.rem(n, owners)
            source_z = z_at(lax.rem(a, 2), a // 2)
            source_core = lax.rem(core + a, NC)
            source = source_z * NC + source_core
            owner = y_at(lax.rem(b, 2), b // 2) * NC + lax.rem(core + b, NC)
            found = table[source * OWNERS_HERE + owner]
            span, row = found // ROWS, lax.rem(found, ROWS)
            tops, crosses = [], []
            for pair in range(PAIRS):
                columns = slice(pair * PAIR, (pair + 1) * PAIR)
                scores = dot(kc[owner, row, :, columns], diagonal(qc[source, span, :, columns]), NT) * SCALE
                grad_p = dot(vc[owner, row, :, columns], diagonal(gc[source, span, :, columns]), NT)
                highest = jnp.max(scores, axis=0, keepdims=True)
                expons = jnp.exp(scores - highest)
                total = jnp.sum(expons, axis=0, keepdims=True)
                cross = jnp.sum(expons * grad_p, axis=0, keepdims=True)
                tops.append(highest + jnp.log(total))
                crosses.append(cross / total)
            part[source_z, source_core, owner, 0] = jnp.concatenate(tops, axis=0)
            part[source_z, source_core, owner, 1] = jnp.concatenate(crosses, axis=0)
            return carry

        lax.fori_loop(0, (last_source - first_source) * owners, one, 0)

    def part_copy(n):
        d, t = n % 2, n // 2
        block = part.at[z_at(d, t), side[d]]
        return remote(block, came.at[z, side[d]], part_s.at[n - 2], part_r.at[n - 2], index_of(y, z_at(d, t), core))

    def arrived(copy, d, a, t, steps):
        copy(d, a, t - 1).wait_recv()
        if t < steps - 1:
            copy(d, a, t).start()

    def each(into, t, act):
        for d in range(2):
            for a in range(2):
                act(into(d, a, t))

    def load(copy):
        copy.start()

    def loaded(copy):
        copy.wait()

    each(z_in, 0, loaded)
    each(y_in, 0, loaded)
    last = 2 * (NZ - 1)
    for t in range(1, NZ):
        ready = 2 * ((t - 1) // 2 + 1)
        ends = t == NZ - 1
        if not ends:
            for d in range(2):
                arrived(z_copy, d, 0, t, NZ)
        if t > 1:
            each(z_in, t - 1, loaded)
        if t > 1 and t % 2 == 1:
            each(y_in, t // 2, loaded)
            part_stats(0, 2 * (t - 1), ready - 2, ready)
        part_stats(2 * (t - 1), 2 * t, 0, ready)
        if ends:
            for n in range(2, last):
                part_copy(n).start()
            for d in range(2):
                arrived(z_copy, d, 0, t, NZ)
        for d in range(2):
            arrived(z_copy, d, 1, t, NZ)
        each(z_in, t, load)
        if t % 2 == 0:
            for a in range(2):
                for d in range(2):
                    arrived(y_copy, d, a, t // 2, NY)
            each(y_in, t // 2, load)
    each(z_in, NZ - 1, loaded)
    part_stats(last, last + 2, 0, 2 * NY)
    for n in range(last, last + 2):
        part_copy(n).start()
    came[z] = part[z]
    for n in range(2, last + 2):
        part_copy(n).wait_recv()

    def merge(n, carry):
        source_core, span = n // CH, lax.rem(n, CH)
        sides = []
        for item in range(NBR):
            r = near_sm[z * NC + source_core, span // 2, 0, lax.rem(span, 2) * NBR + item]
            holder = r // ROWS
            sides.append(came[lax.rem(holder // NC, NZ), source_core,
                              holder // (NC * NZ) * NC + lax.rem(holder, NC)])
        peak = jnp.maximum(sides[0][0], sides[1][0])
        weights = [jnp.exp(one[0] - peak) for one in sides]
        total = weights[0] + weights[1]
        full[z, 0, n] = peak + jnp.log(total)
        full[z, 1, n] = (weights[0] * sides[0][1] + weights[1] * sides[1][1]) / total
        return carry

    lax.fori_loop(0, NC * CH, merge, 0)
    back = [
        remote(full.at[z], full.at[z], full_s.at[s - 1], full_r.at[s - 1], index_of(y, z + s, core))
        for s in range(1, NZ)
    ]
    for copy in back:
        copy.start()
    for copy in back:
        copy.wait_recv()
    for copy in local:
        copy.wait()
    for copy in near_x + near_line + sibling + back:
        copy.wait_send()
    for n in range(2, last + 2):
        part_copy(n).wait_send()
    for d in range(2):
        for a in range(2):
            for t in range(NZ - 1):
                z_copy(d, a, t).wait_send()
            for t in range(NY - 1):
                y_copy(d, a, t).wait_send()


def gather(q, g, k, v, lists):
    sem = pltpu.SemaphoreType.DMA
    vmem = pl.BlockSpec(memory_space=pltpu.VMEM)
    part_shape = (NZ, NC, OWNERS_HERE, 2, PAIRS, HEAD)
    near_shape = (SOURCES, NX, 1, 128)
    near_count = NX - 1 + SOURCES - 1
    return pl.pallas_call(
        gather_kernel,
        out_shape=(
            jax.ShapeDtypeStruct((NZ, NC, CH, SPAN, HALF), bf16),
            jax.ShapeDtypeStruct((NZ, NC, CH, SPAN, HALF), bf16),
            jax.ShapeDtypeStruct((NY, NC, ROWS, NLEN, HALF), bf16),
            jax.ShapeDtypeStruct((NY, NC, ROWS, NLEN, HALF), bf16),
            jax.ShapeDtypeStruct((SOURCES * OWNERS_HERE,), jnp.int32),
            jax.ShapeDtypeStruct((SOURCES * OWNERS_HERE,), jnp.int32),
            jax.ShapeDtypeStruct(STAT_SHAPE, f32),
        ),
        in_specs=[ANY] * 4 + [vmem],
        out_specs=(ANY,) * 4 + (SMEM, SMEM, vmem),
        scratch_shapes=[
            pltpu.VMEM((SOURCES, CH, SPAN, HALF), bf16),
            pltpu.VMEM((SOURCES, CH, SPAN, HALF), bf16),
            pltpu.VMEM((OWNERS_HERE, ROWS, NLEN, HALF), bf16),
            pltpu.VMEM((OWNERS_HERE, ROWS, NLEN, HALF), bf16),
            pltpu.VMEM(near_shape, jnp.int32),
            pltpu.SMEM(near_shape, jnp.int32),
            pltpu.VMEM(part_shape, f32),
            pltpu.VMEM(part_shape, f32),
            sem((4,)),
            sem((4,)),
            sem((4,)),
            sem((2, 2, NZ - 1)),
            sem((2, 2, NZ - 1)),
            sem((2, 2, NY - 1)),
            sem((2, 2, NY - 1)),
            sem((near_count,)),
            sem((near_count,)),
            sem,
            sem((2, 2, NZ)),
            sem((2, 2, NY)),
            sem((2 * NZ - 2,)),
            sem((2 * NZ - 2,)),
            sem((NZ - 1,)),
            sem((NZ - 1,)),
        ],
        compiler_params=pltpu.CompilerParams(
            collective_id=0, has_side_effects=True, vmem_limit_bytes=56 * 2**20),
        name="gather_blocks",
    )(q, g, k, v, lists)


def whole(shape, **more):
    return pl.BlockSpec(shape, lambda *_: (0,) * len(shape), **more)


SMEM = pl.BlockSpec(memory_space=pltpu.SMEM)
ROW_BLOCK = pl.BlockSpec((ROWS, NLEN, HALF), lambda n: (n, 0, 0))
SPAN_BLOCK = whole((SPANS_HERE, SPAN, HALF), pipeline_mode=pl.Buffered(1))
STAT_SHAPE = (NZ, 2, NC * CH, PAIRS, HEAD)


def grads_kernel(table, hits, q, g, k, v, stat, dq, dk, dv, dk_acc, dv_acc):
    owner = pl.program_id(0)

    @pl.when(owner == 0)
    def _():
        def clear(n, carry):
            dq[n] = jnp.zeros((SPAN, HALF), bf16)
            return carry

        lax.fori_loop(0, SPANS_HERE, clear, 0)

    def fresh(n, carry):
        dk_acc[n] = jnp.zeros((NLEN, HALF), f32)
        dv_acc[n] = jnp.zeros((NLEN, HALF), f32)
        return carry

    lax.fori_loop(0, ROWS, fresh, 0)

    def item(source, carry):
        slot = source * OWNERS_HERE + owner

        @pl.when(hits[slot] > 0)
        def _():
            found = table[slot]
            local, row = lax.rem(source, NC) * CH + found // ROWS, lax.rem(found, ROWS)
            span = source * CH + found // ROWS
            log_total = stat[source // NC, 0, local]
            delta = stat[source // NC, 1, local]
            for pair in range(PAIRS):
                columns = slice(pair * PAIR, (pair + 1) * PAIR)
                keys, values = k[row, :, columns], v[row, :, columns]
                queries, grads = diagonal(q[span, :, columns]), diagonal(g[span, :, columns])
                scores = dot(keys, queries, NT) * SCALE
                probs = jnp.exp(scores - log_total[pair:pair + 1])
                grad_p = dot(values, grads, NT)
                grad_s = (probs * (grad_p - delta[pair:pair + 1]) * SCALE).astype(bf16)
                dv_acc[row, :, columns] += dot(probs.astype(bf16), grads, NN)
                dk_acc[row, :, columns] += dot(grad_s, queries, NN)
                more = dot(grad_s, keys, TN)
                more = jnp.concatenate([more[:SPAN, :HEAD], more[SPAN:, HEAD:]], axis=1)
                more = more.astype(bf16).astype(f32)
                dq[span, :, columns] = (dq[span, :, columns].astype(f32) + more).astype(bf16)

        return carry

    lax.fori_loop(0, SOURCES, item, 0)

    def settle(n, carry):
        dk[n] = dk_acc[n].astype(bf16)
        dv[n] = dv_acc[n].astype(bf16)
        return carry

    lax.fori_loop(0, ROWS, settle, 0)


def grads(table, hits, qa, ga, ka, va, stat):
    return pl.pallas_call(
        grads_kernel,
        grid=(OWNERS_HERE,),
        out_shape=(
            jax.ShapeDtypeStruct((SPANS_HERE, SPAN, HALF), bf16),
            jax.ShapeDtypeStruct((ROWS_HERE, NLEN, HALF), bf16),
            jax.ShapeDtypeStruct((ROWS_HERE, NLEN, HALF), bf16),
        ),
        in_specs=[SMEM, SMEM, SPAN_BLOCK, SPAN_BLOCK, ROW_BLOCK, ROW_BLOCK, whole(STAT_SHAPE)],
        out_specs=(whole((SPANS_HERE, SPAN, HALF)), ROW_BLOCK, ROW_BLOCK),
        scratch_shapes=[pltpu.VMEM((ROWS, NLEN, HALF), f32)] * 2,
        compiler_params=pltpu.CompilerParams(vmem_limit_bytes=56 * 2**20),
        name="part_grads",
    )(table, hits, qa, ga, ka, va, stat)


def reduce_kernel(dqp, dkp, dvp, dq, dk, dv, z_in, z_own, y_in, y_own,
                  zl, yl, zs, zr, ys, yr, out_s, out_r, out_l):
    y, z, core = place()
    sib = index_of(y, z, 1 - core)
    z_peer = (index_of(y, z + 1, core), index_of(y, z - 1, core))
    y_peer = (index_of(y + 1, z, core), index_of(y - 1, z, core))
    greet((sib,) + z_peer + y_peer)
    own = pl.ds(pl.multiple_of(core * HALF, HALF), HALF)
    y_src = (dkp, dvp)
    side = (1 - core, core)

    def z_block(d, t):
        return lax.rem(z - 1 - t + 2 * NZ, NZ) if d == 0 else lax.rem(z + 1 + t, NZ)

    def y_block(d, t):
        return lax.rem(y - 1 - t + 2 * NY, NY) if d == 0 else lax.rem(y + 1 + t, NY)

    def z_copy(d, t):
        src = dqp.at[z_block(d, 0), side[d]] if t == 0 else z_in.at[d, t - 1]
        return remote(src, z_in.at[d, t], zs.at[d, t], zr.at[d, t], z_peer[d])

    def y_copy(d, sub, t):
        src = y_src[d].at[y_block(d, 0), side[sub]] if t == 0 else y_in.at[d, sub, t - 1]
        return remote(src, y_in.at[d, sub, t], ys.at[d, sub, t], yr.at[d, sub, t], y_peer[d])

    def z_load(d, t):
        return pltpu.make_async_copy(dqp.at[z_block(d, t + 1), side[d]], z_own.at[d, t], zl.at[d, t])

    def y_load(d, sub, t):
        return pltpu.make_async_copy(
            y_src[d].at[y_block(d, t + 1), side[sub]], y_own.at[d, sub, t], yl.at[d, sub, t])

    for d in range(2):
        y_copy(d, 0, 0).start()
    for d in range(2):
        z_copy(d, 0).start()
    for d in range(2):
        y_copy(d, 1, 0).start()
    for t in range(NY - 1):
        for sub in range(2):
            for d in range(2):
                y_load(d, sub, t).start()
    for t in range(NZ - 1):
        for d in range(2):
            z_load(d, t).start()

    def add(total, more, count):
        def one(n, carry):
            total[n] = (total[n].astype(f32) + more[n].astype(f32)).astype(bf16)
            return carry

        lax.fori_loop(0, count, one, 0)

    def finish(which, out, src):
        there = remote(src[0], out.at[:, :, own], out_s.at[which], out_r.at[which], sib)
        here = pltpu.make_async_copy(src[1], out.at[:, :, own], out_l.at[which])
        return there, here

    ends = (
        finish(0, dk, (y_in.at[0, 0, NY - 2], y_in.at[0, 1, NY - 2])),
        finish(1, dv, (y_in.at[1, 0, NY - 2], y_in.at[1, 1, NY - 2])),
        finish(2, dq, (z_in.at[0, NZ - 2], z_in.at[1, NZ - 2])),
    )

    def z_step(t):
        for d in range(2):
            z_copy(d, t).wait_recv()
            z_load(d, t).wait()
            add(z_in.at[d, t], z_own.at[d, t], CH)
            if t < NZ - 2:
                z_copy(d, t + 1).start()
            else:
                ends[2][d].start()

    def y_step(t, sub):
        for d in range(2):
            y_copy(d, sub, t).wait_recv()
            y_load(d, sub, t).wait()
            add(y_in.at[d, sub, t], y_own.at[d, sub, t], ROWS)
            if t < NY - 2:
                y_copy(d, sub, t + 1).start()
            else:
                ends[d][sub].start()

    z_step(0)
    y_step(0, 0)
    z_step(1)
    y_step(0, 1)
    z_step(2)
    y_step(1, 0)
    z_step(3)
    z_step(4)
    y_step(1, 1)
    z_step(5)
    y_step(2, 0)
    z_step(6)
    y_step(2, 1)
    for there, here in ends:
        there.wait()
        here.wait()
    for d in range(2):
        for t in range(NZ - 1):
            z_copy(d, t).wait_send()
        for sub in range(2):
            for t in range(NY - 1):
                y_copy(d, sub, t).wait_send()


def reduce(dqp, dkp, dvp):
    sem = pltpu.SemaphoreType.DMA
    return pl.pallas_call(
        reduce_kernel,
        out_shape=(
            jax.ShapeDtypeStruct((CH, SPAN, WIDE), bf16),
            jax.ShapeDtypeStruct((ROWS, NLEN, WIDE), bf16),
            jax.ShapeDtypeStruct((ROWS, NLEN, WIDE), bf16),
        ),
        in_specs=[ANY] * 3,
        out_specs=(ANY,) * 3,
        scratch_shapes=[
            pltpu.VMEM((2, NZ - 1, CH, SPAN, HALF), bf16),
            pltpu.VMEM((2, NZ - 1, CH, SPAN, HALF), bf16),
            pltpu.VMEM((2, 2, NY - 1, ROWS, NLEN, HALF), bf16),
            pltpu.VMEM((2, 2, NY - 1, ROWS, NLEN, HALF), bf16),
            sem((2, NZ - 1)),
            sem((2, 2, NY - 1)),
            sem((2, NZ - 1)),
            sem((2, NZ - 1)),
            sem((2, 2, NY - 1)),
            sem((2, 2, NY - 1)),
            sem((3,)),
            sem((3,)),
            sem((3,)),
        ],
        compiler_params=pltpu.CompilerParams(
            collective_id=2, has_side_effects=True, vmem_limit_bytes=56 * 2**20),
        name="reduce_blocks",
    )(dqp, dkp, dvp)


def per_device(queries, out_grad, row_keys, row_values, neighbours):
    few = neighbours.size
    lists = jnp.pad(neighbours.reshape(1, few), ((0, 0), (0, 128 - few)))
    qa, ga, ka, va, table, hits, full = gather(queries, out_grad, row_keys, row_values, lists)
    dqp, dkp, dvp = grads(
        table,
        hits,
        qa.reshape(SPANS_HERE, SPAN, HALF),
        ga.reshape(SPANS_HERE, SPAN, HALF),
        ka.reshape(ROWS_HERE, NLEN, HALF),
        va.reshape(ROWS_HERE, NLEN, HALF),
        full,
    )
    return reduce(
        dqp.reshape(NZ, NC, CH, SPAN, HALF),
        dkp.reshape(NY, NC, ROWS, NLEN, HALF),
        dvp.reshape(NY, NC, ROWS, NLEN, HALF),
    )


def solution(mesh):
    in_specs = (
        P("seq", None, "mp"),
        P("seq", None, "mp"),
        P("seq", None, "mp"),
        P("seq", None, "mp"),
        P(("seq", "mp"), None),
    )
    out_specs = (P("seq", None, "mp"), P("seq", None, "mp"), P("seq", None, "mp"))
    return jax.shard_map(
        per_device, mesh=mesh, in_specs=in_specs, out_specs=out_specs, check_vma=False
    )
```

```python
import jax
import jax.numpy as jnp
from jax import lax
from jax.experimental import pallas as pl
from jax.experimental.pallas import tpu as pltpu
from jax.sharding import PartitionSpec as P

HEAD = 128
UNROLL = 4
SPAN = 64
NLEN = 128
NBR = 2
NX, NY, NZ, NC = 4, 4, 8, 2
CH, ROWS = 8, 8
WIDE = 1024
HALF = WIDE // NC
PAIR = 2 * HEAD
PAIRS = HALF // PAIR
SOURCES = NZ * NC
SPANS_HERE = SOURCES * CH
OWNERS_HERE = NY * NC
ROWS_HERE = OWNERS_HERE * ROWS
SLOTS = SOURCES * OWNERS_HERE
SCALE = HEAD ** (-0.5)
MESH = pl.DeviceIdType.MESH
ANY = pl.BlockSpec(memory_space=pl.ANY)
f32, bf16 = jnp.float32, jnp.bfloat16


def place():
    me = lax.axis_index("seq")
    core = lax.rem(me, NC)
    z = lax.rem(me // NC, NZ)
    y = me // (NC * NZ)
    return y, z, core


def index_of(y, z, core):
    return (lax.rem(y + NY, NY) * NZ + lax.rem(z + NZ, NZ)) * NC + core


def greet(peers):
    barrier = pltpu.get_barrier_semaphore()
    for peer in peers:
        pl.semaphore_signal(barrier, inc=1, device_id={"seq": peer}, device_id_type=MESH)
    pl.semaphore_wait(barrier, len(peers))


def remote(src, dst, send_sem, recv_sem, peer):
    return pltpu.make_async_remote_copy(
        src_ref=src, dst_ref=dst, send_sem=send_sem, recv_sem=recv_sem,
        device_id={"seq": peer}, device_id_type=MESH)


NT = ((1,), (1,))
NN = ((1,), (0,))
TN = ((0,), (0,))


def dot(a, b, dims):
    return lax.dot_general(a, b, (dims, ((), ())), preferred_element_type=f32)


def diagonal(both):
    blank = jnp.zeros((SPAN, HEAD), both.dtype)
    return jnp.concatenate([
        jnp.concatenate([both[:, :HEAD], blank], axis=1),
        jnp.concatenate([blank, both[:, HEAD:]], axis=1),
    ], axis=0)


def gather_kernel(q, g, k, v, lists, qa, ga, ka, va, table, hits, order, same, ends, slots, full,
                  qc, gc, kc, vc, near, near_sm, keys, ranks, part, came,
                  own_l, sib_s, sib_r, zs, zr, ys, yr, near_s, near_r, near_l, z_load, y_load,
                  part_s, part_r, full_s, full_r):
    y, z, core = place()
    mp = lax.axis_index("mp")
    sib = index_of(y, z, 1 - core)
    z_peer = (index_of(y, z + 1, core), index_of(y, z - 1, core))
    y_peer = (index_of(y + 1, z, core), index_of(y - 1, z, core))
    line = [index_of(y, z + s, core) for s in range(1, NZ)]
    line += [index_of(y, z + s, 1 - core) for s in range(NZ)]
    barrier = pltpu.get_barrier_semaphore()
    for s in range(1, NX):
        pl.semaphore_signal(
            barrier, inc=1, device_id={"mp": lax.rem(mp + s, NX)}, device_id_type=MESH)
    for peer in line + list(y_peer):
        pl.semaphore_signal(barrier, inc=1, device_id={"seq": peer}, device_id_type=MESH)
    pl.semaphore_wait(barrier, NX - 1 + len(line) + len(y_peer))
    mine = z * NC + core
    near_x = [
        pltpu.make_async_remote_copy(
            src_ref=lists, dst_ref=near.at[mine, mp], send_sem=near_s.at[s - 1],
            recv_sem=near_r.at[s - 1], device_id={"mp": lax.rem(mp + s, NX)}, device_id_type=MESH)
        for s in range(1, NX)
    ]
    near_line = [
        remote(near.at[mine], near.at[mine], near_s.at[NX - 1 + n], near_r.at[NX - 1 + n], peer)
        for n, peer in enumerate(line)
    ]
    own = pl.ds(pl.multiple_of(core * HALF, HALF), HALF)
    other = pl.ds(pl.multiple_of((1 - core) * HALF, HALF), HALF)
    sources = (q, g, k, v)
    gathered = (qa, ga, ka, va)
    here = (qc, gc, kc, vc)
    side = (core, 1 - core)

    def z_at(d, t):
        return lax.rem(z + (2 * d - 1) * t + NZ, NZ)

    def y_at(d, t):
        return lax.rem(y + (2 * d - 1) * t + NY, NY)

    def z_copy(d, a, t):
        dst = gathered[a].at[z_at(d, t), side[d]]
        src = sources[a].at[:, :, own] if (t == 0 and d == 0) else dst
        return remote(src, dst, zs.at[d, a, t], zr.at[d, a, t], z_peer[d])

    def y_copy(d, a, t):
        dst = gathered[2 + a].at[y_at(d, t), side[d]]
        src = sources[2 + a].at[:, :, own] if (t == 0 and d == 0) else dst
        return remote(src, dst, ys.at[d, a, t], yr.at[d, a, t], y_peer[d])

    def z_in(d, a, t):
        src = sources[a].at[:, :, own] if (t == 0 and d == 0) else gathered[a].at[z_at(d, t), side[d]]
        return pltpu.make_async_copy(src, here[a].at[z_at(d, t) * NC + side[d]], z_load.at[d, a, t])

    def y_in(d, a, t):
        src = sources[2 + a].at[:, :, own] if (t == 0 and d == 0) else gathered[2 + a].at[y_at(d, t), side[d]]
        return pltpu.make_async_copy(src, here[2 + a].at[y_at(d, t) * NC + side[d]], y_load.at[d, a, t])

    at = (z, z, y, y)
    sibling = [
        remote(sources[a].at[:, :, other], gathered[a].at[at[a], core], sib_s.at[a], sib_r.at[a], sib)
        for a in range(4)
    ]
    for copy in near_x:
        copy.start()
    for a in range(2):
        z_copy(0, a, 0).start()
    for copy in sibling[:2]:
        copy.start()
    for a in range(2):
        y_copy(0, a, 0).start()
    for copy in sibling[2:]:
        copy.start()
    local = [
        pltpu.make_async_copy(sources[a].at[:, :, own], gathered[a].at[at[a], core], own_l.at[a])
        for a in range(4)
    ]
    for copy in local:
        copy.start()
    for a in range(2):
        z_in(0, a, 0).start()
        y_in(0, a, 0).start()
    near[mine, mp] = lists[...]
    for a in range(2):
        sibling[a].wait_recv()
        z_copy(1, a, 0).start()
        z_in(1, a, 0).start()
    for a in range(2):
        sibling[2 + a].wait_recv()
        y_copy(1, a, 0).start()
        y_in(1, a, 0).start()
    listed = pltpu.make_async_copy(near, near_sm, near_l)

    def look_up(slot, carry):
        source, owner = slot // OWNERS_HERE, lax.rem(slot, OWNERS_HERE)
        wanted = ((owner // NC) * NZ + z) * NC + lax.rem(owner, NC)
        found = jnp.int32(0)
        hit = jnp.int32(0)
        for item in range(CH * NBR):
            r = near_sm[source, item // (CH * NBR // NX), 0, item % (CH * NBR // NX)]
            same = (r // ROWS == wanted).astype(jnp.int32)
            found = found + same * (item // NBR * ROWS + lax.rem(r, ROWS) - found)
            hit = hit + same
        table[slot] = found
        hit = (hit > 0).astype(jnp.int32)
        hits[slot] = hit
        none = ROWS * SOURCES
        keys[owner * SOURCES + source] = source + none + hit * (lax.rem(found, ROWS) * SOURCES - none)
        return carry

    def rank(n, carry):
        first = n // SOURCES * SOURCES
        mine = keys[n]
        below = jnp.int32(0)
        for other_one in range(SOURCES):
            below = below + (keys[first + other_one] < mine).astype(jnp.int32)
        ranks[n] = below
        return carry

    def put_in_order(n, carry):
        first, at_n = n // SOURCES * SOURCES, lax.rem(n, SOURCES)
        chosen = jnp.int32(0)
        for one in range(SOURCES):
            chosen = chosen + one * (ranks[first + one] == at_n).astype(jnp.int32)
        order[n] = chosen
        return carry

    def mark_same(n, carry):
        first, at_n = n // SOURCES * SOURCES, lax.rem(n, SOURCES)
        now = keys[first + order[n]] // SOURCES
        before = keys[first + order[first + lax.rem(at_n + SOURCES - 1, SOURCES)]] // SOURCES
        same[n] = (now == before).astype(jnp.int32) * ((at_n + SOURCES - 1) // SOURCES)
        return carry

    def mark_end(n, carry):
        first, row = n // ROWS * SOURCES, lax.rem(n, ROWS)
        below = jnp.int32(0)
        upto = jnp.int32(0)
        for one in range(SOURCES):
            key = keys[first + one]
            below = below + (key < row * SOURCES).astype(jnp.int32)
            upto = upto + (key < (row + 1) * SOURCES).astype(jnp.int32)
        ends[n] = upto * (upto > below).astype(jnp.int32)
        return carry

    def mark_slot(n, carry):
        source, item = n // (CH * NBR), lax.rem(n, CH * NBR)
        each_x = CH * NBR // NX
        holder = near_sm[source, item // each_x, 0, lax.rem(item, each_x)] // ROWS
        local = (lax.rem(holder // NC, NZ) == z).astype(jnp.int32)
        first = (holder // (NC * NZ) * NC + lax.rem(holder, NC)) * SOURCES
        slots[n] = SLOTS + local * (first + ranks[first + source] - SLOTS)
        return carry

    def part_stats(first_source, last_source, first_owner, last_owner):
        owners = last_owner - first_owner

        def one(n):
            a = first_source + n // owners
            b = first_owner + lax.rem(n, owners)
            source_z = z_at(lax.rem(a, 2), a // 2)
            source_core = lax.rem(core + a, NC)
            source = source_z * NC + source_core
            owner = y_at(lax.rem(b, 2), b // 2) * NC + lax.rem(core + b, NC)
            found = table[source * OWNERS_HERE + owner]
            span, row = found // ROWS, lax.rem(found, ROWS)
            tops, crosses = [], []
            for pair in range(PAIRS):
                columns = slice(pair * PAIR, (pair + 1) * PAIR)
                scores = dot(kc[owner, row, :, columns], diagonal(qc[source, span, :, columns]), NT) * SCALE
                grad_p = dot(vc[owner, row, :, columns], diagonal(gc[source, span, :, columns]), NT)
                highest = jnp.max(scores, axis=0, keepdims=True)
                expons = jnp.exp(scores - highest)
                total = jnp.sum(expons, axis=0, keepdims=True)
                cross = jnp.sum(expons * grad_p, axis=0, keepdims=True)
                tops.append(highest + jnp.log(total))
                crosses.append(cross / total)
            return source_z, source_core, owner, tops, crosses

        def some(n, carry):
            results = [one(2 * n + more) for more in range(2)]
            for source_z, source_core, owner, tops, crosses in results:
                part[source_z, source_core, owner, 0] = jnp.concatenate(tops, axis=0)
                part[source_z, source_core, owner, 1] = jnp.concatenate(crosses, axis=0)
            return carry

        lax.fori_loop(0, (last_source - first_source) * owners // 2, some, 0)

    def part_copy(n):
        d, t = n % 2, n // 2
        block = part.at[z_at(d, t), side[d]]
        return remote(block, came.at[z, side[d]], part_s.at[n - 2], part_r.at[n - 2], index_of(y, z_at(d, t), core))

    def arrived(copy, d, a, t, steps):
        copy(d, a, t - 1).wait_recv()
        if t < steps - 1:
            copy(d, a, t).start()

    def each(into, t, act):
        for d in range(2):
            for a in range(2):
                act(into(d, a, t))

    def load(copy):
        copy.start()

    def loaded(copy):
        copy.wait()

    each(z_in, 0, loaded)
    each(y_in, 0, loaded)
    last = 2 * (NZ - 1)
    for t in range(1, NZ):
        ready = 2 * ((t - 1) // 2 + 1)
        final = t == NZ - 1
        if not final:
            for d in range(2):
                arrived(z_copy, d, 0, t, NZ)
        if t > 1:
            each(z_in, t - 1, loaded)
        if t == 1:
            for copy in near_x:
                copy.wait_recv()
            for copy in near_line:
                copy.start()
        elif t == 2:
            for copy in near_line:
                copy.wait_recv()
            listed.start()
            listed.wait()
            lax.fori_loop(0, SLOTS // 2, look_up, 0)
        else:
            if t % 2 == 1:
                each(y_in, t // 2, loaded)
                part_stats(0, 2 * (t - 1), ready - 2, ready)
            if t == 3:
                part_stats(0, 4, 0, 2)
            part_stats(2 * (t - 1), 2 * t, 0, ready)
        if final:
            for n in range(2, last):
                part_copy(n).start()
            for d in range(2):
                arrived(z_copy, d, 0, t, NZ)
        for d in range(2):
            arrived(z_copy, d, 1, t, NZ)
        each(z_in, t, load)
        if t % 2 == 0:
            for a in range(2):
                for d in range(2):
                    arrived(y_copy, d, a, t // 2, NY)
            each(y_in, t // 2, load)
        if t == 2:
            lax.fori_loop(SLOTS // 2, SLOTS, look_up, 0)
        elif t == 3:
            lax.fori_loop(0, SLOTS, rank, 0)
        elif t == 4:
            lax.fori_loop(0, SLOTS, put_in_order, 0)
        elif t == 5:
            lax.fori_loop(0, SLOTS, mark_same, 0)
            lax.fori_loop(0, ROWS_HERE, mark_end, 0)
        elif t == 6:
            lax.fori_loop(0, SPANS_HERE * NBR, mark_slot, 0)
    each(z_in, NZ - 1, loaded)
    part_stats(last, last + 2, 0, 2 * NY)
    for n in range(last, last + 2):
        part_copy(n).start()
    came[z] = part[z]
    for n in range(2, last + 2):
        part_copy(n).wait_recv()

    def merge(n, carry):
        source_core, span = n // CH, lax.rem(n, CH)
        sides = []
        for item in range(NBR):
            r = near_sm[z * NC + source_core, span // 2, 0, lax.rem(span, 2) * NBR + item]
            holder = r // ROWS
            sides.append(came[lax.rem(holder // NC, NZ), source_core,
                              holder // (NC * NZ) * NC + lax.rem(holder, NC)])
        peak = jnp.maximum(sides[0][0], sides[1][0])
        weights = [jnp.exp(one[0] - peak) for one in sides]
        total = weights[0] + weights[1]
        full[z, 0, n] = peak + jnp.log(total)
        full[z, 1, n] = (weights[0] * sides[0][1] + weights[1] * sides[1][1]) / total
        return carry

    lax.fori_loop(0, NC * CH, merge, 0)
    back = [
        remote(full.at[z], full.at[z], full_s.at[s - 1], full_r.at[s - 1], index_of(y, z + s, core))
        for s in range(1, NZ)
    ]
    for copy in back:
        copy.start()
    for copy in back:
        copy.wait_recv()
    for copy in local:
        copy.wait()
    for copy in near_x + near_line + sibling + back:
        copy.wait_send()
    for n in range(2, last + 2):
        part_copy(n).wait_send()
    for d in range(2):
        for a in range(2):
            for t in range(NZ - 1):
                z_copy(d, a, t).wait_send()
            for t in range(NY - 1):
                y_copy(d, a, t).wait_send()


def gather(q, g, k, v, lists):
    sem = pltpu.SemaphoreType.DMA
    vmem = pl.BlockSpec(memory_space=pltpu.VMEM)
    part_shape = (NZ, NC, OWNERS_HERE, 2, PAIRS, HEAD)
    near_shape = (SOURCES, NX, 1, 128)
    near_count = NX - 1 + SOURCES - 1
    return pl.pallas_call(
        gather_kernel,
        out_shape=(
            jax.ShapeDtypeStruct((NZ, NC, CH, SPAN, HALF), bf16),
            jax.ShapeDtypeStruct((NZ, NC, CH, SPAN, HALF), bf16),
            jax.ShapeDtypeStruct((NY, NC, ROWS, NLEN, HALF), bf16),
            jax.ShapeDtypeStruct((NY, NC, ROWS, NLEN, HALF), bf16),
            jax.ShapeDtypeStruct((SLOTS,), jnp.int32),
            jax.ShapeDtypeStruct((SLOTS,), jnp.int32),
            jax.ShapeDtypeStruct((SLOTS,), jnp.int32),
            jax.ShapeDtypeStruct((SLOTS,), jnp.int32),
            jax.ShapeDtypeStruct((ROWS_HERE,), jnp.int32),
            jax.ShapeDtypeStruct((SPANS_HERE * NBR,), jnp.int32),
            jax.ShapeDtypeStruct(STAT_SHAPE, f32),
        ),
        in_specs=[ANY] * 4 + [vmem],
        out_specs=(ANY,) * 4 + (SMEM,) * 6 + (vmem,),
        scratch_shapes=[
            pltpu.VMEM((SOURCES, CH, SPAN, HALF), bf16),
            pltpu.VMEM((SOURCES, CH, SPAN, HALF), bf16),
            pltpu.VMEM((OWNERS_HERE, ROWS, NLEN, HALF), bf16),
            pltpu.VMEM((OWNERS_HERE, ROWS, NLEN, HALF), bf16),
            pltpu.VMEM(near_shape, jnp.int32),
            pltpu.SMEM(near_shape, jnp.int32),
            pltpu.SMEM((SLOTS,), jnp.int32),
            pltpu.SMEM((SLOTS,), jnp.int32),
            pltpu.VMEM(part_shape, f32),
            pltpu.VMEM(part_shape, f32),
            sem((4,)),
            sem((4,)),
            sem((4,)),
            sem((2, 2, NZ - 1)),
            sem((2, 2, NZ - 1)),
            sem((2, 2, NY - 1)),
            sem((2, 2, NY - 1)),
            sem((near_count,)),
            sem((near_count,)),
            sem,
            sem((2, 2, NZ)),
            sem((2, 2, NY)),
            sem((2 * NZ - 2,)),
            sem((2 * NZ - 2,)),
            sem((NZ - 1,)),
            sem((NZ - 1,)),
        ],
        compiler_params=pltpu.CompilerParams(
            collective_id=0, has_side_effects=True, vmem_limit_bytes=56 * 2**20),
        name="gather_blocks",
    )(q, g, k, v, lists)


SMEM = pl.BlockSpec(memory_space=pltpu.SMEM)
STAT_SHAPE = (NZ, 2, NC * CH, PAIRS, HEAD)


def grads_kernel(qa, ga, ka, va, table, hits, order, same, ends, slots, stat, dq, dk, dv,
                 qv, gv, k0, v0, k1, v1, dk_sum, dv_sum, y_own, y_in, parts, z_out, z_in,
                 span_l, row_l, zs, zr, ys, yr, out_s, out_r, out_l):
    y, z, core = place()
    sib = index_of(y, z, 1 - core)
    z_peer = (index_of(y, z + 1, core), index_of(y, z - 1, core))
    y_peer = (index_of(y + 1, z, core), index_of(y - 1, z, core))
    side = (1 - core, core)
    units = [(p, t, d) for p in range(PAIRS) for t in range(NY) for d in range(2)]
    row_bufs = ((k0, v0), (k1, v1))

    def z_block(d, t):
        return lax.rem(z + (2 * d - 1) * (1 + t) + NZ, NZ)

    def y_block(d, t):
        return lax.rem(y + (2 * d - 1) * (1 + t) + NY, NY)

    def span_load(p):
        columns = slice(p * PAIR, (p + 1) * PAIR)
        return [
            pltpu.make_async_copy(src.at[:, :, :, :, columns], dst, span_l.at[p, n])
            for n, (src, dst) in enumerate(((qa, qv), (ga, gv)))
        ]

    def row_load(u):
        p, t, d = units[u]
        columns = slice(p * PAIR, (p + 1) * PAIR)
        return [
            pltpu.make_async_copy(
                src.at[y_block(d, t), side[d], :, :, columns], row_bufs[u % 2][n], row_l.at[u, n])
            for n, src in enumerate((ka, va))
        ]

    for copy in row_load(0) + span_load(0):
        copy.start()
    greet((sib,) + z_peer + y_peer)
    dk_sum[0] = jnp.zeros((NLEN, PAIR), f32)
    dv_sum[0] = jnp.zeros((NLEN, PAIR), f32)
    for p in range(PAIRS):
        parts[p, SLOTS] = jnp.zeros((SPAN, PAIR), bf16)

    def compute(u):
        p, t, d = units[u]
        keys_ref, values_ref = row_bufs[u % 2]
        owner = y_block(d, t) * NC + side[d]
        for copy in row_load(u):
            copy.wait()
        if u + 1 < len(units):
            for copy in row_load(u + 1):
                copy.start()

        def slot(n):
            source = order[owner * SOURCES + n]
            found = table[source * OWNERS_HERE + owner]
            empty = 1 - hits[source * OWNERS_HERE + owner]
            span, row = found // ROWS, lax.rem(found, ROWS)
            local = lax.rem(source, NC) * CH + span
            log_total = stat[source // NC, 0, local][p:p + 1] + empty.astype(f32) * 1e30
            delta = stat[source // NC, 1, local][p:p + 1]
            keys, values = keys_ref[row], values_ref[row]
            queries = diagonal(qv[source // NC, lax.rem(source, NC), span])
            grads = diagonal(gv[source // NC, lax.rem(source, NC), span])
            probs = jnp.exp(dot(keys, queries, NT) * SCALE - log_total)
            grad_p = dot(values, grads, NT)
            grad_s = (probs * (grad_p - delta) * SCALE).astype(bf16)
            more = dot(grad_s, keys, TN)
            more = jnp.concatenate([more[:SPAN, :HEAD], more[SPAN:, HEAD:]], axis=1)
            return dot(probs.astype(bf16), grads, NN), dot(grad_s, queries, NN), more.astype(bf16)

        def step(i, carry):
            results = [slot(i * UNROLL + n) for n in range(UNROLL)]
            for n, (dv_part, dk_part, more) in enumerate(results):
                at_n = i * UNROLL + n
                parts[p, owner * SOURCES + at_n] = more
                go_on = same[owner * SOURCES + at_n].astype(f32)
                dv_sum[at_n + 1] = dv_part + go_on * dv_sum[at_n]
                dk_sum[at_n + 1] = dk_part + go_on * dk_sum[at_n]
            return carry

        lax.fori_loop(0, SOURCES // UNROLL, step, 0)

        def settle(row, carry):
            at_row = ends[owner * ROWS + row]
            y_own[p, d, t, 0, row] = dk_sum[at_row].astype(bf16)
            y_own[p, d, t, 1, row] = dv_sum[at_row].astype(bf16)
            return carry

        lax.fori_loop(0, ROWS, settle, 0)
        if t == 0:
            y_copy(p, d, 0).start()

    def y_copy(p, d, t):
        src = y_own.at[p, d, 0] if t == 0 else y_in.at[p, d, t - 1]
        return remote(src, y_in.at[p, d, t], ys.at[p, d, t], yr.at[p, d, t], y_peer[d])

    def z_copy(p, d, t):
        src = z_out.at[p, d] if t == 0 else z_in.at[p, d, t - 1]
        return remote(src, z_in.at[p, d, t], zs.at[p, d, t], zr.at[p, d, t], z_peer[d])

    def finish(p, which):
        columns = pl.ds(pl.multiple_of(core * HALF + p * PAIR, PAIR), PAIR)
        out = (dk, dv, dq)[which].at[:, :, columns]
        if which < 2:
            src = (y_in.at[p, 0, NY - 2, which], y_in.at[p, 1, NY - 2, which])
        else:
            src = (z_in.at[p, 0, NZ - 2], z_in.at[p, 1, NZ - 2])
        return (
            remote(src[0], out, out_s.at[p, which], out_r.at[p, which], sib),
            pltpu.make_async_copy(src[1], out, out_l.at[p, which]),
        )

    def y_step(p, t):
        for d in range(2):
            y_copy(p, d, t).wait_recv()

            def add(n, carry):
                for a in range(2):
                    total = y_in[p, d, t, a, n].astype(f32) + y_own[p, d, t + 1, a, n].astype(f32)
                    y_in[p, d, t, a, n] = total.astype(bf16)
                return carry

            lax.fori_loop(0, ROWS, add, 0)
            if t < NY - 2:
                y_copy(p, d, t + 1).start()
            else:
                finish(p, 0)[d].start()
                finish(p, 1)[d].start()

    def span_part(p, d, t, n):
        item = ((z_block(d, t) * NC + side[d]) * CH + n) * NBR
        return parts[p, slots[item]].astype(f32) + parts[p, slots[item + 1]].astype(f32)

    def z_begin(p):
        for d in range(2):
            def fill(n, carry):
                z_out[p, d, n] = span_part(p, d, 0, n).astype(bf16)
                return carry

            lax.fori_loop(0, CH, fill, 0)
            z_copy(p, d, 0).start()

    def z_step(p, t):
        for d in range(2):
            z_copy(p, d, t).wait_recv()

            def add(n, carry):
                z_in[p, d, t, n] = (z_in[p, d, t, n].astype(f32) + span_part(p, d, t + 1, n)).astype(bf16)
                return carry

            lax.fori_loop(0, CH, add, 0)
            if t < NZ - 2:
                z_copy(p, d, t + 1).start()
            else:
                finish(p, 2)[d].start()

    for copy in span_load(0):
        copy.wait()
    for u in range(6):
        compute(u)
    y_step(0, 0)
    compute(6)
    compute(7)
    for copy in span_load(1):
        copy.start()
    z_begin(0)
    for copy in span_load(1):
        copy.wait()
    compute(8)
    z_step(0, 0)
    compute(9)
    z_step(0, 1)
    y_step(0, 1)
    compute(10)
    z_step(0, 2)
    compute(11)
    z_step(0, 3)
    compute(12)
    z_step(0, 4)
    compute(13)
    z_step(0, 5)
    y_step(0, 2)
    compute(14)
    z_step(0, 6)
    compute(15)
    z_begin(1)
    y_step(1, 0)
    z_step(1, 0)
    z_step(1, 1)
    z_step(1, 2)
    y_step(1, 1)
    z_step(1, 3)
    z_step(1, 4)
    z_step(1, 5)
    z_step(1, 6)
    y_step(1, 2)
    for p in range(PAIRS):
        for which in range(3):
            there, here = finish(p, which)
            there.wait()
            here.wait()
        for d in range(2):
            for t in range(NZ - 1):
                z_copy(p, d, t).wait_send()
            for t in range(NY - 1):
                y_copy(p, d, t).wait_send()


def grads(qa, ga, ka, va, tables, stat):
    sem = pltpu.SemaphoreType.DMA
    vmem = pltpu.VMEM
    rows = vmem((ROWS, NLEN, PAIR), bf16)
    return pl.pallas_call(
        grads_kernel,
        out_shape=(
            jax.ShapeDtypeStruct((CH, SPAN, WIDE), bf16),
            jax.ShapeDtypeStruct((ROWS, NLEN, WIDE), bf16),
            jax.ShapeDtypeStruct((ROWS, NLEN, WIDE), bf16),
        ),
        in_specs=[ANY] * 4 + [SMEM] * len(tables) + [pl.BlockSpec(memory_space=vmem)],
        out_specs=(ANY,) * 3,
        scratch_shapes=[
            vmem((NZ, NC, CH, SPAN, PAIR), bf16),
            vmem((NZ, NC, CH, SPAN, PAIR), bf16),
            rows,
            rows,
            rows,
            rows,
            vmem((SOURCES + 1, NLEN, PAIR), f32),
            vmem((SOURCES + 1, NLEN, PAIR), f32),
            vmem((PAIRS, 2, NY, 2, ROWS, NLEN, PAIR), bf16),
            vmem((PAIRS, 2, NY - 1, 2, ROWS, NLEN, PAIR), bf16),
            vmem((PAIRS, SLOTS + 1, SPAN, PAIR), bf16),
            vmem((PAIRS, 2, CH, SPAN, PAIR), bf16),
            vmem((PAIRS, 2, NZ - 1, CH, SPAN, PAIR), bf16),
            sem((PAIRS, 2)),
            sem((PAIRS * NY * 2, 2)),
            sem((PAIRS, 2, NZ - 1)),
            sem((PAIRS, 2, NZ - 1)),
            sem((PAIRS, 2, NY - 1)),
            sem((PAIRS, 2, NY - 1)),
            sem((PAIRS, 3)),
            sem((PAIRS, 3)),
            sem((PAIRS, 3)),
        ],
        compiler_params=pltpu.CompilerParams(
            collective_id=1, has_side_effects=True, vmem_limit_bytes=62 * 2**20),
        name="grads_and_sums",
    )(qa, ga, ka, va, *tables, stat)


def per_device(queries, out_grad, row_keys, row_values, neighbours):
    few = neighbours.size
    lists = jnp.pad(neighbours.reshape(1, few), ((0, 0), (0, 128 - few)))
    qa, ga, ka, va, *tables, full = gather(queries, out_grad, row_keys, row_values, lists)
    return grads(qa, ga, ka, va, tables, full)


def solution(mesh):
    in_specs = (
        P("seq", None, "mp"),
        P("seq", None, "mp"),
        P("seq", None, "mp"),
        P("seq", None, "mp"),
        P(("seq", "mp"), None),
    )
    out_specs = (P("seq", None, "mp"), P("seq", None, "mp"), P("seq", None, "mp"))
    return jax.shard_map(
        per_device, mesh=mesh, in_specs=in_specs, out_specs=out_specs, check_vma=False
    )
```

```python
import jax
import jax.numpy as jnp
from jax import lax
from jax.experimental import pallas as pl
from jax.experimental.pallas import tpu as pltpu
from jax.sharding import PartitionSpec as P

HEAD = 128
UNROLL = 8
SPAN = 64
NLEN = 128
NBR = 2
NX, NY, NZ, NC = 4, 4, 8, 2
CH, ROWS = 8, 8
WIDE = 1024
HALF = WIDE // NC
PAIR = 2 * HEAD
PAIRS = HALF // PAIR
SOURCES = NZ * NC
SPANS_HERE = SOURCES * CH
OWNERS_HERE = NY * NC
ROWS_HERE = OWNERS_HERE * ROWS
SLOTS = SOURCES * OWNERS_HERE
SCALE = HEAD ** (-0.5)
MESH = pl.DeviceIdType.MESH
ANY = pl.BlockSpec(memory_space=pl.ANY)
f32, bf16 = jnp.float32, jnp.bfloat16


def place():
    me = lax.axis_index("seq")
    core = lax.rem(me, NC)
    z = lax.rem(me // NC, NZ)
    y = me // (NC * NZ)
    return y, z, core


def index_of(y, z, core):
    return (lax.rem(y + NY, NY) * NZ + lax.rem(z + NZ, NZ)) * NC + core


def greet(peers):
    barrier = pltpu.get_barrier_semaphore()
    for peer in peers:
        pl.semaphore_signal(barrier, inc=1, device_id={"seq": peer}, device_id_type=MESH)
    pl.semaphore_wait(barrier, len(peers))


def remote(src, dst, send_sem, recv_sem, peer):
    return pltpu.make_async_remote_copy(
        src_ref=src, dst_ref=dst, send_sem=send_sem, recv_sem=recv_sem,
        device_id={"seq": peer}, device_id_type=MESH)


NT = ((1,), (1,))
NN = ((1,), (0,))
TN = ((0,), (0,))


def dot(a, b, dims):
    return lax.dot_general(a, b, (dims, ((), ())), preferred_element_type=f32)


def diagonal(both):
    blank = jnp.zeros((SPAN, HEAD), both.dtype)
    return jnp.concatenate([
        jnp.concatenate([both[:, :HEAD], blank], axis=1),
        jnp.concatenate([blank, both[:, HEAD:]], axis=1),
    ], axis=0)


def gather_kernel(q, g, k, v, lists, qa, ga, ka, va, table, hits, order, same, ends, slots, full,
                  qc, gc, kc, vc, near, near_sm, keys, ranks, part, came,
                  own_l, sib_s, sib_r, zs, zr, ys, yr, near_s, near_r, near_l, z_load, y_load,
                  part_s, part_r, full_s, full_r):
    y, z, core = place()
    mp = lax.axis_index("mp")
    sib = index_of(y, z, 1 - core)
    z_peer = (index_of(y, z + 1, core), index_of(y, z - 1, core))
    y_peer = (index_of(y + 1, z, core), index_of(y - 1, z, core))
    line = [index_of(y, z + s, core) for s in range(1, NZ)]
    line += [index_of(y, z + s, 1 - core) for s in range(NZ)]
    barrier = pltpu.get_barrier_semaphore()
    for s in range(1, NX):
        pl.semaphore_signal(
            barrier, inc=1, device_id={"mp": lax.rem(mp + s, NX)}, device_id_type=MESH)
    for peer in line + list(y_peer):
        pl.semaphore_signal(barrier, inc=1, device_id={"seq": peer}, device_id_type=MESH)
    pl.semaphore_wait(barrier, NX - 1 + len(line) + len(y_peer))
    mine = z * NC + core
    near_x = [
        pltpu.make_async_remote_copy(
            src_ref=lists, dst_ref=near.at[mine, mp], send_sem=near_s.at[s - 1],
            recv_sem=near_r.at[s - 1], device_id={"mp": lax.rem(mp + s, NX)}, device_id_type=MESH)
        for s in range(1, NX)
    ]
    near_line = [
        remote(near.at[mine], near.at[mine], near_s.at[NX - 1 + n], near_r.at[NX - 1 + n], peer)
        for n, peer in enumerate(line)
    ]
    own = pl.ds(pl.multiple_of(core * HALF, HALF), HALF)
    other = pl.ds(pl.multiple_of((1 - core) * HALF, HALF), HALF)
    sources = (q, g, k, v)
    gathered = (qa, ga, ka, va)
    here = (qc, gc, kc, vc)
    side = (core, 1 - core)

    def z_at(d, t):
        return lax.rem(z + (2 * d - 1) * t + NZ, NZ)

    def y_at(d, t):
        return lax.rem(y + (2 * d - 1) * t + NY, NY)

    def z_copy(d, a, t):
        dst = gathered[a].at[z_at(d, t), side[d]]
        src = sources[a].at[:, :, own] if (t == 0 and d == 0) else dst
        return remote(src, dst, zs.at[d, a, t], zr.at[d, a, t], z_peer[d])

    def y_copy(d, a, t):
        dst = gathered[2 + a].at[y_at(d, t), side[d]]
        src = sources[2 + a].at[:, :, own] if (t == 0 and d == 0) else dst
        return remote(src, dst, ys.at[d, a, t], yr.at[d, a, t], y_peer[d])

    def z_in(d, a, t):
        src = sources[a].at[:, :, own] if (t == 0 and d == 0) else gathered[a].at[z_at(d, t), side[d]]
        return pltpu.make_async_copy(src, here[a].at[z_at(d, t) * NC + side[d]], z_load.at[d, a, t])

    def y_in(d, a, t):
        src = sources[2 + a].at[:, :, own] if (t == 0 and d == 0) else gathered[2 + a].at[y_at(d, t), side[d]]
        return pltpu.make_async_copy(src, here[2 + a].at[y_at(d, t) * NC + side[d]], y_load.at[d, a, t])

    at = (z, z, y, y)
    sibling = [
        remote(sources[a].at[:, :, other], gathered[a].at[at[a], core], sib_s.at[a], sib_r.at[a], sib)
        for a in range(4)
    ]
    for copy in near_x:
        copy.start()
    for a in range(2):
        z_copy(0, a, 0).start()
    for copy in sibling[:2]:
        copy.start()
    for a in range(2):
        y_copy(0, a, 0).start()
    for copy in sibling[2:]:
        copy.start()
    local = [
        pltpu.make_async_copy(sources[a].at[:, :, own], gathered[a].at[at[a], core], own_l.at[a])
        for a in range(4)
    ]
    for copy in local:
        copy.start()
    for a in range(2):
        z_in(0, a, 0).start()
        y_in(0, a, 0).start()
    near[mine, mp] = lists[...]
    for a in range(2):
        sibling[a].wait_recv()
        z_copy(1, a, 0).start()
        z_in(1, a, 0).start()
    for a in range(2):
        sibling[2 + a].wait_recv()
        y_copy(1, a, 0).start()
        y_in(1, a, 0).start()
    listed = pltpu.make_async_copy(near, near_sm, near_l)

    def look_up(slot, carry):
        source, owner = slot // OWNERS_HERE, lax.rem(slot, OWNERS_HERE)
        wanted = ((owner // NC) * NZ + z) * NC + lax.rem(owner, NC)
        found = jnp.int32(0)
        hit = jnp.int32(0)
        for item in range(CH * NBR):
            r = near_sm[source, item // (CH * NBR // NX), 0, item % (CH * NBR // NX)]
            same = (r // ROWS == wanted).astype(jnp.int32)
            found = found + same * (item // NBR * ROWS + lax.rem(r, ROWS) - found)
            hit = hit + same
        table[slot] = found
        hit = (hit > 0).astype(jnp.int32)
        hits[slot] = hit
        none = ROWS * SOURCES
        keys[owner * SOURCES + source] = source + none + hit * (lax.rem(found, ROWS) * SOURCES - none)
        return carry

    def rank(n, carry):
        first = n // SOURCES * SOURCES
        mine = keys[n]
        below = jnp.int32(0)
        for other_one in range(SOURCES):
            below = below + (keys[first + other_one] < mine).astype(jnp.int32)
        ranks[n] = below
        return carry

    def put_in_order(n, carry):
        first, at_n = n // SOURCES * SOURCES, lax.rem(n, SOURCES)
        chosen = jnp.int32(0)
        for one in range(SOURCES):
            chosen = chosen + one * (ranks[first + one] == at_n).astype(jnp.int32)
        order[n] = chosen
        return carry

    def mark_same(n, carry):
        first, at_n = n // SOURCES * SOURCES, lax.rem(n, SOURCES)
        now = keys[first + order[n]] // SOURCES
        before = keys[first + order[first + lax.rem(at_n + SOURCES - 1, SOURCES)]] // SOURCES
        same[n] = (now == before).astype(jnp.int32) * ((at_n + SOURCES - 1) // SOURCES)
        return carry

    def mark_end(n, carry):
        first, row = n // ROWS * SOURCES, lax.rem(n, ROWS)
        below = jnp.int32(0)
        upto = jnp.int32(0)
        for one in range(SOURCES):
            key = keys[first + one]
            below = below + (key < row * SOURCES).astype(jnp.int32)
            upto = upto + (key < (row + 1) * SOURCES).astype(jnp.int32)
        ends[n] = upto * (upto > below).astype(jnp.int32)
        return carry

    def mark_slot(n, carry):
        source, item = n // (CH * NBR), lax.rem(n, CH * NBR)
        each_x = CH * NBR // NX
        holder = near_sm[source, item // each_x, 0, lax.rem(item, each_x)] // ROWS
        local = (lax.rem(holder // NC, NZ) == z).astype(jnp.int32)
        first = (holder // (NC * NZ) * NC + lax.rem(holder, NC)) * SOURCES
        slots[n] = SLOTS + local * (first + ranks[first + source] - SLOTS)
        return carry

    def part_stats(first_source, last_source, first_owner, last_owner):
        owners = last_owner - first_owner

        def one(n):
            a = first_source + n // owners
            b = first_owner + lax.rem(n, owners)
            source_z = z_at(lax.rem(a, 2), a // 2)
            source_core = lax.rem(core + a, NC)
            source = source_z * NC + source_core
            owner = y_at(lax.rem(b, 2), b // 2) * NC + lax.rem(core + b, NC)
            found = table[source * OWNERS_HERE + owner]
            span, row = found // ROWS, lax.rem(found, ROWS)
            tops, crosses = [], []
            for pair in range(PAIRS):
                columns = slice(pair * PAIR, (pair + 1) * PAIR)
                scores = dot(kc[owner, row, :, columns], diagonal(qc[source, span, :, columns]), NT) * SCALE
                grad_p = dot(vc[owner, row, :, columns], diagonal(gc[source, span, :, columns]), NT)
                highest = jnp.max(scores, axis=0, keepdims=True)
                expons = jnp.exp(scores - highest)
                total = jnp.sum(expons, axis=0, keepdims=True)
                cross = jnp.sum(expons * grad_p, axis=0, keepdims=True)
                tops.append(highest + jnp.log(total))
                crosses.append(cross / total)
            return source_z, source_core, owner, tops, crosses

        def some(n, carry):
            results = [one(2 * n + more) for more in range(2)]
            for source_z, source_core, owner, tops, crosses in results:
                part[source_z, source_core, owner, 0] = jnp.concatenate(tops, axis=0)
                part[source_z, source_core, owner, 1] = jnp.concatenate(crosses, axis=0)
            return carry

        lax.fori_loop(0, (last_source - first_source) * owners // 2, some, 0)

    def part_copy(n):
        d, t = n % 2, n // 2
        block = part.at[z_at(d, t), side[d]]
        return remote(block, came.at[z, side[d]], part_s.at[n - 2], part_r.at[n - 2], index_of(y, z_at(d, t), core))

    def arrived(copy, d, a, t, steps):
        copy(d, a, t - 1).wait_recv()
        if t < steps - 1:
            copy(d, a, t).start()

    def each(into, t, act):
        for d in range(2):
            for a in range(2):
                act(into(d, a, t))

    def load(copy):
        copy.start()

    def loaded(copy):
        copy.wait()

    each(z_in, 0, loaded)
    each(y_in, 0, loaded)
    last = 2 * (NZ - 1)
    for t in range(1, NZ):
        ready = 2 * ((t - 1) // 2 + 1)
        final = t == NZ - 1
        if not final:
            for d in range(2):
                arrived(z_copy, d, 0, t, NZ)
        if t > 1:
            each(z_in, t - 1, loaded)
        if t == 1:
            for copy in near_x:
                copy.wait_recv()
            for copy in near_line:
                copy.start()
        elif t == 2:
            for copy in near_line:
                copy.wait_recv()
            listed.start()
            listed.wait()
            lax.fori_loop(0, SLOTS // 2, look_up, 0)
        else:
            if t % 2 == 1:
                each(y_in, t // 2, loaded)
                part_stats(0, 2 * (t - 1), ready - 2, ready)
            if t == 3:
                part_stats(0, 4, 0, 2)
            part_stats(2 * (t - 1), 2 * t, 0, ready)
        if final:
            for n in range(2, last):
                part_copy(n).start()
            for d in range(2):
                arrived(z_copy, d, 0, t, NZ)
                z_in(d, 0, t).start()
        for d in range(2):
            arrived(z_copy, d, 1, t, NZ)
            if final:
                z_in(d, 1, t).start()
        if not final:
            each(z_in, t, load)
        if t % 2 == 0:
            for a in range(2):
                for d in range(2):
                    arrived(y_copy, d, a, t // 2, NY)
            each(y_in, t // 2, load)
        if t == 2:
            lax.fori_loop(SLOTS // 2, SLOTS, look_up, 0)
        elif t == 3:
            lax.fori_loop(0, SLOTS, rank, 0)
        elif t == 4:
            lax.fori_loop(0, SLOTS, put_in_order, 0)
        elif t == 5:
            lax.fori_loop(0, SLOTS, mark_same, 0)
            lax.fori_loop(0, ROWS_HERE, mark_end, 0)
        elif t == 6:
            lax.fori_loop(0, SPANS_HERE * NBR, mark_slot, 0)
    each(z_in, NZ - 1, loaded)
    part_stats(last, last + 2, 0, 2 * NY)
    for n in range(last, last + 2):
        part_copy(n).start()
    came[z] = part[z]
    for n in range(2, last + 2):
        part_copy(n).wait_recv()

    def merge(n):
        source_core, span = n // CH, n % CH
        sides = []
        for item in range(NBR):
            r = near_sm[z * NC + source_core, span // 2, 0, (span % 2) * NBR + item]
            holder = r // ROWS
            sides.append(came[lax.rem(holder // NC, NZ), source_core,
                              holder // (NC * NZ) * NC + lax.rem(holder, NC)])
        peak = jnp.maximum(sides[0][0], sides[1][0])
        weights = [jnp.exp(one[0] - peak) for one in sides]
        total = weights[0] + weights[1]
        full[z, 0, n] = peak + jnp.log(total)
        full[z, 1, n] = (weights[0] * sides[0][1] + weights[1] * sides[1][1]) / total

    for n in range(NC * CH):
        merge(n)
    back = [
        remote(full.at[z], full.at[z], full_s.at[s - 1], full_r.at[s - 1], index_of(y, z + s, core))
        for s in range(1, NZ)
    ]
    for copy in back:
        copy.start()
    for copy in back:
        copy.wait_recv()
    for copy in local:
        copy.wait()
    for copy in near_x + near_line + sibling + back:
        copy.wait_send()
    for n in range(2, last + 2):
        part_copy(n).wait_send()
    for d in range(2):
        for a in range(2):
            for t in range(NZ - 1):
                z_copy(d, a, t).wait_send()
            for t in range(NY - 1):
                y_copy(d, a, t).wait_send()


def gather(q, g, k, v, lists):
    sem = pltpu.SemaphoreType.DMA
    vmem = pl.BlockSpec(memory_space=pltpu.VMEM)
    part_shape = (NZ, NC, OWNERS_HERE, 2, PAIRS, HEAD)
    near_shape = (SOURCES, NX, 1, 128)
    near_count = NX - 1 + SOURCES - 1
    return pl.pallas_call(
        gather_kernel,
        out_shape=(
            jax.ShapeDtypeStruct((NZ, NC, CH, SPAN, HALF), bf16),
            jax.ShapeDtypeStruct((NZ, NC, CH, SPAN, HALF), bf16),
            jax.ShapeDtypeStruct((NY, NC, ROWS, NLEN, HALF), bf16),
            jax.ShapeDtypeStruct((NY, NC, ROWS, NLEN, HALF), bf16),
            jax.ShapeDtypeStruct((SLOTS,), jnp.int32),
            jax.ShapeDtypeStruct((SLOTS,), jnp.int32),
            jax.ShapeDtypeStruct((SLOTS,), jnp.int32),
            jax.ShapeDtypeStruct((SLOTS,), jnp.int32),
            jax.ShapeDtypeStruct((ROWS_HERE,), jnp.int32),
            jax.ShapeDtypeStruct((SPANS_HERE * NBR,), jnp.int32),
            jax.ShapeDtypeStruct(STAT_SHAPE, f32),
        ),
        in_specs=[ANY] * 4 + [vmem],
        out_specs=(ANY,) * 4 + (SMEM,) * 6 + (vmem,),
        scratch_shapes=[
            pltpu.VMEM((SOURCES, CH, SPAN, HALF), bf16),
            pltpu.VMEM((SOURCES, CH, SPAN, HALF), bf16),
            pltpu.VMEM((OWNERS_HERE, ROWS, NLEN, HALF), bf16),
            pltpu.VMEM((OWNERS_HERE, ROWS, NLEN, HALF), bf16),
            pltpu.VMEM(near_shape, jnp.int32),
            pltpu.SMEM(near_shape, jnp.int32),
            pltpu.SMEM((SLOTS,), jnp.int32),
            pltpu.SMEM((SLOTS,), jnp.int32),
            pltpu.VMEM(part_shape, f32),
            pltpu.VMEM(part_shape, f32),
            sem((4,)),
            sem((4,)),
            sem((4,)),
            sem((2, 2, NZ - 1)),
            sem((2, 2, NZ - 1)),
            sem((2, 2, NY - 1)),
            sem((2, 2, NY - 1)),
            sem((near_count,)),
            sem((near_count,)),
            sem,
            sem((2, 2, NZ)),
            sem((2, 2, NY)),
            sem((2 * NZ - 2,)),
            sem((2 * NZ - 2,)),
            sem((NZ - 1,)),
            sem((NZ - 1,)),
        ],
        compiler_params=pltpu.CompilerParams(
            collective_id=0, has_side_effects=True, vmem_limit_bytes=56 * 2**20),
        name="gather_blocks",
    )(q, g, k, v, lists)


SMEM = pl.BlockSpec(memory_space=pltpu.SMEM)
STAT_SHAPE = (NZ, 2, NC * CH, PAIRS, HEAD)


def grads_kernel(qa, ga, ka, va, table, hits, order, same, ends, slots, stat, dq, dk, dv,
                 qv, gv, k0, v0, k1, v1, dk_sum, dv_sum, y_own, y_in, parts, z_out, z_in,
                 span_l, row_l, zs, zr, ys, yr, out_s, out_r, out_l):
    y, z, core = place()
    sib = index_of(y, z, 1 - core)
    z_peer = (index_of(y, z + 1, core), index_of(y, z - 1, core))
    y_peer = (index_of(y + 1, z, core), index_of(y - 1, z, core))
    side = (1 - core, core)
    units = [(p, t, d) for p in range(PAIRS) for t in range(NY) for d in range(2)]
    row_bufs = ((k0, v0), (k1, v1))

    def z_block(d, t):
        return lax.rem(z + (2 * d - 1) * (1 + t) + NZ, NZ)

    def y_block(d, t):
        return lax.rem(y + (2 * d - 1) * (1 + t) + NY, NY)

    def span_load(p):
        columns = slice(p * PAIR, (p + 1) * PAIR)
        return [
            pltpu.make_async_copy(src.at[:, :, :, :, columns], dst, span_l.at[p, n])
            for n, (src, dst) in enumerate(((qa, qv), (ga, gv)))
        ]

    def row_load(u):
        p, t, d = units[u]
        columns = slice(p * PAIR, (p + 1) * PAIR)
        return [
            pltpu.make_async_copy(
                src.at[y_block(d, t), side[d], :, :, columns], row_bufs[u % 2][n], row_l.at[u, n])
            for n, src in enumerate((ka, va))
        ]

    for copy in row_load(0) + span_load(0):
        copy.start()
    greet((sib,) + z_peer + y_peer)
    dk_sum[0] = jnp.zeros((NLEN, PAIR), f32)
    dv_sum[0] = jnp.zeros((NLEN, PAIR), f32)
    for p in range(PAIRS):
        parts[p, SLOTS] = jnp.zeros((SPAN, PAIR), bf16)

    def compute(u):
        p, t, d = units[u]
        keys_ref, values_ref = row_bufs[u % 2]
        owner = y_block(d, t) * NC + side[d]
        for copy in row_load(u):
            copy.wait()
        if u + 1 < len(units):
            for copy in row_load(u + 1):
                copy.start()

        def slot(n):
            source = order[owner * SOURCES + n]
            found = table[source * OWNERS_HERE + owner]
            empty = 1 - hits[source * OWNERS_HERE + owner]
            span, row = found // ROWS, lax.rem(found, ROWS)
            local = lax.rem(source, NC) * CH + span
            log_total = stat[source // NC, 0, local][p:p + 1] + empty.astype(f32) * 1e30
            delta = stat[source // NC, 1, local][p:p + 1]
            keys, values = keys_ref[row], values_ref[row]
            queries = diagonal(qv[source // NC, lax.rem(source, NC), span])
            grads = diagonal(gv[source // NC, lax.rem(source, NC), span])
            probs = jnp.exp(dot(keys, queries, NT) * SCALE - log_total)
            grad_p = dot(values, grads, NT)
            grad_s = (probs * (grad_p - delta) * SCALE).astype(bf16)
            more = dot(grad_s, keys, TN)
            more = jnp.concatenate([more[:SPAN, :HEAD], more[SPAN:, HEAD:]], axis=1)
            return dot(probs.astype(bf16), grads, NN), dot(grad_s, queries, NN), more.astype(bf16)

        def step(i, carry):
            results = [slot(i * UNROLL + n) for n in range(UNROLL)]
            for n, (dv_part, dk_part, more) in enumerate(results):
                at_n = i * UNROLL + n
                parts[p, owner * SOURCES + at_n] = more
                go_on = same[owner * SOURCES + at_n].astype(f32)
                dv_sum[at_n + 1] = dv_part + go_on * dv_sum[at_n]
                dk_sum[at_n + 1] = dk_part + go_on * dk_sum[at_n]
            return carry

        lax.fori_loop(0, SOURCES // UNROLL, step, 0)

        def settle(row, carry):
            at_row = ends[owner * ROWS + row]
            y_own[p, d, t, 0, row] = dk_sum[at_row].astype(bf16)
            y_own[p, d, t, 1, row] = dv_sum[at_row].astype(bf16)
            return carry

        lax.fori_loop(0, ROWS, settle, 0)
        if t == 0:
            y_copy(p, d, 0).start()

    def y_copy(p, d, t):
        src = y_own.at[p, d, 0] if t == 0 else y_in.at[p, d, t - 1]
        return remote(src, y_in.at[p, d, t], ys.at[p, d, t], yr.at[p, d, t], y_peer[d])

    def z_copy(p, d, t):
        src = z_out.at[p, d] if t == 0 else z_in.at[p, d, t - 1]
        return remote(src, z_in.at[p, d, t], zs.at[p, d, t], zr.at[p, d, t], z_peer[d])

    def finish(p, which):
        columns = pl.ds(pl.multiple_of(core * HALF + p * PAIR, PAIR), PAIR)
        out = (dk, dv, dq)[which].at[:, :, columns]
        if which < 2:
            src = (y_in.at[p, 0, NY - 2, which], y_in.at[p, 1, NY - 2, which])
        else:
            src = (z_in.at[p, 0, NZ - 2], z_in.at[p, 1, NZ - 2])
        return (
            remote(src[0], out, out_s.at[p, which], out_r.at[p, which], sib),
            pltpu.make_async_copy(src[1], out, out_l.at[p, which]),
        )

    def y_step(p, t):
        for d in range(2):
            y_copy(p, d, t).wait_recv()

            def add(n, carry):
                for a in range(2):
                    total = y_in[p, d, t, a, n].astype(f32) + y_own[p, d, t + 1, a, n].astype(f32)
                    y_in[p, d, t, a, n] = total.astype(bf16)
                return carry

            lax.fori_loop(0, ROWS, add, 0)
            if t < NY - 2:
                y_copy(p, d, t + 1).start()
            else:
                finish(p, 0)[d].start()
                finish(p, 1)[d].start()

    def span_part(p, d, t, n):
        item = ((z_block(d, t) * NC + side[d]) * CH + n) * NBR
        return parts[p, slots[item]].astype(f32) + parts[p, slots[item + 1]].astype(f32)

    def z_begin(p):
        for d in range(2):
            def fill(n, carry):
                z_out[p, d, n] = span_part(p, d, 0, n).astype(bf16)
                return carry

            lax.fori_loop(0, CH, fill, 0)
            z_copy(p, d, 0).start()

    def z_step(p, t):
        for d in range(2):
            z_copy(p, d, t).wait_recv()

            def add(n, carry):
                z_in[p, d, t, n] = (z_in[p, d, t, n].astype(f32) + span_part(p, d, t + 1, n)).astype(bf16)
                return carry

            lax.fori_loop(0, CH, add, 0)
            if t < NZ - 2:
                z_copy(p, d, t + 1).start()
            else:
                finish(p, 2)[d].start()

    for copy in span_load(0):
        copy.wait()
    for u in range(6):
        compute(u)
    y_step(0, 0)
    compute(6)
    compute(7)
    for copy in span_load(1):
        copy.start()
    z_begin(0)
    for copy in span_load(1):
        copy.wait()
    compute(8)
    compute(9)
    compute(10)
    z_step(0, 0)
    y_step(0, 1)
    compute(11)
    compute(12)
    compute(13)
    z_step(0, 1)
    compute(14)
    compute(15)
    z_begin(1)
    z_step(0, 2)
    y_step(1, 0)
    z_step(1, 0)
    z_step(0, 3)
    y_step(0, 2)
    z_step(1, 1)
    z_step(0, 4)
    z_step(1, 2)
    z_step(0, 5)
    y_step(1, 1)
    z_step(1, 3)
    z_step(0, 6)
    z_step(1, 4)
    z_step(1, 5)
    z_step(1, 6)
    y_step(1, 2)
    for p in range(PAIRS):
        for which in range(3):
            there, here = finish(p, which)
            there.wait()
            here.wait()
        for d in range(2):
            for t in range(NZ - 1):
                z_copy(p, d, t).wait_send()
            for t in range(NY - 1):
                y_copy(p, d, t).wait_send()


def grads(qa, ga, ka, va, tables, stat):
    sem = pltpu.SemaphoreType.DMA
    vmem = pltpu.VMEM
    rows = vmem((ROWS, NLEN, PAIR), bf16)
    return pl.pallas_call(
        grads_kernel,
        out_shape=(
            jax.ShapeDtypeStruct((CH, SPAN, WIDE), bf16),
            jax.ShapeDtypeStruct((ROWS, NLEN, WIDE), bf16),
            jax.ShapeDtypeStruct((ROWS, NLEN, WIDE), bf16),
        ),
        in_specs=[ANY] * 4 + [SMEM] * len(tables) + [pl.BlockSpec(memory_space=vmem)],
        out_specs=(ANY,) * 3,
        scratch_shapes=[
            vmem((NZ, NC, CH, SPAN, PAIR), bf16),
            vmem((NZ, NC, CH, SPAN, PAIR), bf16),
            rows,
            rows,
            rows,
            rows,
            vmem((SOURCES + 1, NLEN, PAIR), f32),
            vmem((SOURCES + 1, NLEN, PAIR), f32),
            vmem((PAIRS, 2, NY, 2, ROWS, NLEN, PAIR), bf16),
            vmem((PAIRS, 2, NY - 1, 2, ROWS, NLEN, PAIR), bf16),
            vmem((PAIRS, SLOTS + 1, SPAN, PAIR), bf16),
            vmem((PAIRS, 2, CH, SPAN, PAIR), bf16),
            vmem((PAIRS, 2, NZ - 1, CH, SPAN, PAIR), bf16),
            sem((PAIRS, 2)),
            sem((PAIRS * NY * 2, 2)),
            sem((PAIRS, 2, NZ - 1)),
            sem((PAIRS, 2, NZ - 1)),
            sem((PAIRS, 2, NY - 1)),
            sem((PAIRS, 2, NY - 1)),
            sem((PAIRS, 3)),
            sem((PAIRS, 3)),
            sem((PAIRS, 3)),
        ],
        compiler_params=pltpu.CompilerParams(
            collective_id=1, has_side_effects=True, vmem_limit_bytes=62 * 2**20),
        name="grads_and_sums",
    )(qa, ga, ka, va, *tables, stat)


def per_device(queries, out_grad, row_keys, row_values, neighbours):
    few = neighbours.size
    lists = jnp.pad(neighbours.reshape(1, few), ((0, 0), (0, 128 - few)))
    qa, ga, ka, va, *tables, full = gather(queries, out_grad, row_keys, row_values, lists)
    return grads(qa, ga, ka, va, tables, full)


def solution(mesh):
    in_specs = (
        P("seq", None, "mp"),
        P("seq", None, "mp"),
        P("seq", None, "mp"),
        P("seq", None, "mp"),
        P(("seq", "mp"), None),
    )
    out_specs = (P("seq", None, "mp"), P("seq", None, "mp"), P("seq", None, "mp"))
    return jax.shard_map(
        per_device, mesh=mesh, in_specs=in_specs, out_specs=out_specs, check_vma=False
    )
```
